128 devices in a mesh: dp: 32 (over z, y, x_hi), mp: 4 (over x_lo, core).
Axes of the slice: x: 4 (x_hi: 2, x_lo: 2; x = x_hi * 2 + x_lo), y: 4, z: 4, core: 2. Of those that a mesh axis runs over, the one named last changes fastest.
Arguments:
- tokens: bfloat16 [16384, 8192], P(('dp', 'mp')), may hold values from -24 to 24
- gain: float32 [8192], replicated, may hold values from 0.1 to 1.9
- query: bfloat16 [16384, 8192], P('dp', 'mp'), may hold values from -64 to 64
- query_tangent: bfloat16 [16384, 8192], P('dp', 'mp'), may hold values from -6 to 6
- kv_weight: bfloat16 [2, 8192, 1024], P(None, 'dp', 'mp'), may hold values from -0.0625 to 0.0625
- kv_bias: float32 [2, 1024], P(None, 'mp'), may hold values from -3 to 3
- kv_task: bfloat16 [2, 8192, 1024], P(None, 'dp', 'mp'), may hold values from -0.0625 to 0.0625
- kv_bias_task: float32 [2, 1024], P(None, 'mp'), may hold values from -3 to 3
- cotangent: bfloat16 [16384, 8192], P('dp', 'mp'), may hold values from -0.046875 to 0.046875
Outputs:
- context: bfloat16 [16384, 8192], P('dp', 'mp')
- context_tangent: bfloat16 [16384, 8192], P('dp', 'mp')
- kv_grad: float32 [2, 8192, 1024], P(None, 'dp', 'mp')
- kv_bias_grad: float32 [2, 1024], P(None, 'mp')
The draws below stay inside these ranges and needn't reach their ends.
All inputs are finite; a program needn't handle non-finite values.
Results may differ from the reference program's by a relative error of at most 0.03.
The reference program's roundings to bfloat16 on the way count: a program that leaves them out, or rounds other values in their place, can miss the bound.
Values may be sent and summed in bfloat16 or wider, within the bound.
A program may use at most 192 MiB of HBM per device.

```python
import jax
import jax.numpy as jnp
from jax import lax

D = 8192
KV_HEADS = 8
HEAD = 128
SEQ = 512
TOKENS = 16384
GROUP = 8
QW = 8192
KVW = 1024
N_DP = 32


def draw_query(key, part):
    key = jax.random.fold_in(key, 7)
    first = jax.random.fold_in(key, 0)
    normal_part = jax.random.normal(first, (TOKENS, QW), jnp.float32)
    return jnp.clip(normal_part, -8.0, 8.0).astype(jnp.bfloat16)


def spiked(drawn, stream_key, source, target, blocks, factor):
    def block_of(dim):
        return (jnp.arange(drawn.shape[dim]) // (drawn.shape[dim] // blocks)).reshape((-1,) + (1,) * (drawn.ndim - 1 - dim))

    near = jax.random.permutation(stream_key, blocks)[block_of(target)]
    other_side = (block_of(target) + blocks // 2) % blocks
    return jnp.where((block_of(source) == near) | (block_of(source) == other_side), factor * drawn, drawn)


def shard_levels(stream_key, dims, cuts, smallest, high):
    level, own = 1.0, jax.random.fold_in(stream_key, 6)
    for axis_at, parts in cuts:
        heights = jnp.exp(jax.random.uniform(jax.random.fold_in(own, axis_at), (parts,), jnp.float32, smallest / len(cuts), high / len(cuts)))
        level = level * jnp.repeat(heights, dims[axis_at] // parts).reshape([-1 if axis == axis_at else 1 for axis in range(len(dims))])
    return level


def centred(key, dims, scale, bound, cuts=(), kind=jnp.bfloat16):
    values = jax.random.normal(key, dims, jnp.float32) * scale
    if len(cuts) > 0:
        values = shard_levels(key, dims, cuts, -0.22, 0.18) * values
    return jnp.clip(values, min=-bound, max=bound).astype(kind)


def gaussian_with(own_key, extent, scale, most, cuts, heavy, dtype=jnp.bfloat16):
    result = scale * jax.random.normal(own_key, extent, jnp.float32)
    if cuts:
        result = result * shard_levels(own_key, extent, cuts, -0.22, 0.18)
    return jnp.clip(spiked(result, jax.random.fold_in(own_key, 3), *heavy), -most, most).astype(dtype)


def setup_inputs(seed: int = 0) -> dict:
    key_of = jax.random.split(jax.random.key(seed), 10)
    tokens = gaussian_with(key_of[0], (TOKENS, D), 1.0, 24.0, ((0, 128),), (0, 1, 128, 5.5))
    gain = jnp.clip(1.0 + 0.18 * jax.random.normal(key_of[1], (D,), jnp.float32), 0.1, 1.9)
    query = draw_query(jax.random.fold_in(key_of[9], 71), 0)
    query_tangent = centred(key_of[3], (TOKENS, QW), 1.0, 6.0, ((0, 32), (1, 4)))
    kv_weight = centred(key_of[4], (2, D, KVW), D ** -0.5, 0.0625, ((1, 32), (2, 4)))
    kv_bias = centred(key_of[5], (2, KVW), 0.5, 3.0, ((1, 4),), jnp.float32)
    kv_task = centred(key_of[6], (2, D, KVW), D ** -0.5, 0.0625, ((1, 32), (2, 4)))
    kv_bias_task = centred(key_of[7], (2, KVW), 0.5, 3.0, ((1, 4),), jnp.float32)
    cotangent = centred(key_of[8], (TOKENS, QW), (TOKENS ** -0.5), 0.046875, ((0, 32), (1, 4)))
    return dict(tokens=tokens, gain=gain, query=query, query_tangent=query_tangent, kv_weight=kv_weight, kv_bias=kv_bias, kv_task=kv_task, kv_bias_task=kv_bias_task, cotangent=cotangent)


def rotate(field, sign):
    length = field.shape[0]
    width = field.shape[-1]
    half_width = width // 2
    position = jnp.arange(length).astype(jnp.float32)
    frequency = jnp.power(1000000.0, -2.0 * jnp.arange(half_width).astype(jnp.float32) / width)
    angle = position[:, None] * frequency[None, :]
    angle = jnp.concatenate([angle, angle], axis=-1)
    cosine = jnp.cos(angle)[:, None, :]
    sine = sign * jnp.sin(angle)[:, None, :]
    turned = jnp.concatenate([-field[..., half_width:], field[..., :half_width]], axis=-1)
    return field * cosine + turned * sine

def multiply(form, left, right):
    return jnp.einsum(form, left.astype(jnp.float32), right.astype(jnp.float32))

def attend(queries, query_tangent, cotangent, keys, values, key_tangent, value_tangent):
    factor = HEAD ** (-0.5)
    length = queries.shape[0]
    causal = jnp.arange(length)[:, None] >= jnp.arange(length)[None, :]
    scores = multiply('tkgh,skh->kgts', queries, keys) * factor
    scores = jnp.where(causal, scores, -jnp.inf)
    highest = lax.optimization_barrier(jnp.max(scores, axis=-1, keepdims=True))
    raised = jnp.exp(scores - highest)
    weights = raised / lax.optimization_barrier(jnp.sum(raised, axis=-1, keepdims=True))
    weights16 = weights.astype(jnp.bfloat16)
    context = multiply('kgts,skh->tkgh', weights16, values)
    spread = (multiply('tkgh,skh->kgts', query_tangent, keys) + multiply('tkgh,skh->kgts', queries, key_tangent)) * factor
    moved = weights * (spread - lax.optimization_barrier(jnp.sum(weights * spread, axis=-1, keepdims=True)))
    moved16 = moved.astype(jnp.bfloat16)
    context_tangent = multiply('kgts,skh->tkgh', moved16, values) + multiply('kgts,skh->tkgh', weights16, value_tangent)
    value_back = multiply('kgts,tkgh->skh', weights16, cotangent)
    pulled = multiply('tkgh,skh->kgts', cotangent, values)
    score_back = (weights * (pulled - lax.optimization_barrier(jnp.sum(weights * pulled, axis=-1, keepdims=True))) * factor).astype(jnp.bfloat16)
    key_turned = multiply('kgts,tkgh->skh', score_back, queries)
    return (context, context_tangent, key_turned, value_back)

def reference(tokens, gain, query, query_tangent, kv_weight, kv_bias, kv_task, kv_bias_task, cotangent):
    wide = tokens.astype(jnp.float32)
    normed = (wide * lax.rsqrt(lax.optimization_barrier(jnp.mean(wide * wide, axis=-1, keepdims=True)) + 1e-06) * gain).astype(jnp.bfloat16)
    base_weight = kv_weight.astype(jnp.float32)
    task_weight = kv_task.astype(jnp.float32)
    grouped = (N_DP, SEQ, KV_HEADS, GROUP, HEAD)
    inputs = (normed.reshape(N_DP, SEQ, D), query.reshape(grouped), query_tangent.reshape(grouped), cotangent.reshape(grouped))

    def group_step(grad_total, pieces):
        rows_normed, rows_query, rows_tangent, rows_cotangent = pieces
        flat = rows_normed.astype(jnp.float32)
        base_kv = jnp.einsum('td,kdc->ktc', flat, base_weight) + kv_bias[:, None, :]
        task_kv = jnp.einsum('td,kdc->ktc', flat, task_weight) + kv_bias_task[:, None, :]
        heads_shape = (SEQ, KV_HEADS, HEAD)
        keys = rotate(base_kv[0].reshape(heads_shape), 1.0).astype(jnp.bfloat16)
        values = base_kv[1].reshape(heads_shape).astype(jnp.bfloat16)
        key_tangent = rotate(task_kv[0].reshape(heads_shape), 1.0).astype(jnp.bfloat16)
        value_tangent = task_kv[1].reshape(heads_shape).astype(jnp.bfloat16)
        context, context_tangent, key_turned, value_back = attend(rows_query, rows_tangent, rows_cotangent, keys, values, key_tangent, value_tangent)
        key_back = rotate(key_turned, -1.0).reshape(SEQ, KVW)
        back16 = jnp.stack([key_back, value_back.reshape(SEQ, KVW)]).astype(jnp.bfloat16)
        back_wide = back16.astype(jnp.float32)
        grad_total = grad_total + jnp.einsum('td,ktc->kdc', flat, back_wide)
        bias_part = lax.optimization_barrier(jnp.sum(back_wide, axis=1))
        return (grad_total, (context.reshape(SEQ, QW).astype(jnp.bfloat16), context_tangent.reshape(SEQ, QW).astype(jnp.bfloat16), bias_part))
    start_grad = jnp.zeros((2, D, KVW), jnp.float32)
    kv_grad, outputs = lax.scan(group_step, start_grad, inputs)
    context = outputs[0].reshape(TOKENS, QW)
    context_tangent = outputs[1].reshape(TOKENS, QW)
    kv_bias_grad = lax.optimization_barrier(jnp.sum(outputs[2], axis=0))
    return (context, context_tangent, kv_grad, kv_bias_grad)
```

```python
import functools

import jax
import jax.numpy as jnp
from jax import lax
from jax.experimental import pallas as pl
from jax.experimental.pallas import tpu as pltpu
from jax.sharding import PartitionSpec as P

HEAD = 128
MESH = pl.DeviceIdType.MESH


class Place:
    def __init__(self):
        dp = lax.axis_index("dp")
        self.mp = lax.axis_index("mp")
        self.z, self.y, self.h = dp // 8, (dp // 2) % 4, dp % 2
        self.dp = dp

    def index(self, kind, along, across, half):
        dy, dz = (along, across) if kind == 0 else (across, along)
        return ((self.z + dz + 4) % 4) * 8 + ((self.y + dy + 4) % 4) * 2 + half

    def device(self, kind, along, across):
        return (self.index(kind, along, across, self.h), self.mp)

    def partner(self):
        return (self.dp + 1 - 2 * self.h, self.mp)

    def core_partner(self):
        return (self.dp, self.mp + 1 - 2 * (self.mp % 2))

    def pair_chip(self):
        return (self.dp, (self.mp + 2) % 4)


def greet(devices):
    barrier = pltpu.get_barrier_semaphore()
    for device in devices:
        pl.semaphore_signal(barrier, inc=1, device_id=device, device_id_type=MESH)
    pl.semaphore_wait(barrier, len(devices))


def ring_devices(place):
    return [
        place.device(0, 1, 0),
        place.device(0, -1, 0),
        place.device(0, 0, 1),
        place.device(0, 0, -1),
        place.partner(),
    ]


class Gather:
    def __init__(self, place, whole, send, recv):
        self.place, self.whole, self.send, self.recv = place, whole, send, recv
        self.slots = [0, 0]
        self.started = []

    def shard(self, kind, index):
        return self.whole.at[kind, pl.ds(pl.multiple_of(index * 256, 256), 256), :]

    def copy(self, kind, index, device, slot):
        block = self.shard(kind, index)
        return pltpu.make_async_remote_copy(
            src_ref=block,
            dst_ref=block,
            send_sem=self.send.at[kind, slot],
            recv_sem=self.recv.at[kind, index],
            device_id=device,
            device_id_type=MESH,
        )

    def start(self, kind, index, device):
        slot = self.slots[kind]
        self.slots[kind] += 1
        copy = self.copy(kind, index, device, slot)
        copy.start()
        self.started.append(copy)

    def wait(self, kind, index):
        self.copy(kind, index, self.place.partner(), 0).wait_recv()

    def spread(self, kind, index, along):
        if along:
            self.start(kind, index, self.place.device(kind, 1, 0))
            self.start(kind, index, self.place.device(kind, -1, 0))
        self.start(kind, index, self.place.device(kind, 0, 1))
        self.start(kind, index, self.place.device(kind, 0, -1))

    def first(self):
        own = self.place.dp
        for kind in range(2):
            self.start(kind, own, self.place.partner())
        for kind in range(2):
            self.spread(kind, own, True)

    def events(self):
        place = self.place

        def partner(kind):
            other = place.index(kind, 0, 0, 1 - place.h)
            self.wait(kind, other)
            self.spread(kind, other, True)

        def side(kind, along):
            near, far = (0, 1) if along < 0 else (1, 0)
            index = place.index(kind, along, 0, near)
            self.wait(kind, index)
            self.start(kind, index, place.device(kind, -along, 0))
            self.spread(kind, index, False)
            index = place.index(kind, along, 0, far)
            self.wait(kind, index)
            self.spread(kind, index, False)

        def opposite(kind):
            for half in range(2):
                index = place.index(kind, 2, 0, half)
                self.wait(kind, index)
                self.spread(kind, index, False)

        def across(kind, along, step):
            near, far = (0, 1) if step < 0 else (1, 0)
            index = place.index(kind, along, step, near)
            self.wait(kind, index)
            self.start(kind, index, place.device(kind, 0, -step))
            self.wait(kind, place.index(kind, along, step, far))

        def across_opposite(kind, along):
            for half in range(2):
                self.wait(kind, place.index(kind, along, 2, half))

        result = []

        def add(blocks, function, *rest):
            for kind in range(2):
                result.append((kind, blocks, functools.partial(function, kind, *rest)))

        add([(0, 0)], partner)
        add([(-1, 0)], side, -1)
        add([(1, 0)], side, 1)
        add([(0, -1)], across, 0, -1)
        add([(0, 1)], across, 0, 1)
        add([(2, 0)], opposite)
        for along in (-1, 1, 2):
            add([(along, -1)], across, along, -1)
            add([(along, 1)], across, along, 1)
            before = {-1: 0, 1: -1, 2: 1}[along]
            add([(before, 2)], across_opposite, before)
        add([(2, 2)], across_opposite, 2)
        return result

    def finish(self):
        for copy in self.started:
            copy.wait_send()


GATHER_SEMS = [pltpu.SemaphoreType.DMA((2, 31)), pltpu.SemaphoreType.DMA((2, 32))]
CHUNK = 32


class Rows:
    def __init__(self, place, whole, send, recv):
        self.place, self.whole, self.send, self.recv = place, whole, send, recv
        self.started = []

    def copy(self, owner, chunk, device, lane):
        rows = pl.multiple_of(owner * 128 + chunk * CHUNK, CHUNK)
        block = self.whole.at[pl.ds(rows, CHUNK), :]
        return pltpu.make_async_remote_copy(
            src_ref=block,
            dst_ref=block,
            send_sem=self.send.at[lane, chunk],
            recv_sem=self.recv.at[owner, chunk],
            device_id=device,
            device_id_type=MESH,
        )

    def start(self, owner, chunk, device, lane):
        copy = self.copy(owner, chunk, device, lane)
        copy.start()
        self.started.append(copy)

    def own(self, chunk):
        self.start(self.place.mp, chunk, self.place.pair_chip(), 0)
        self.start(self.place.mp, chunk, self.place.core_partner(), 1)

    def wait(self, owner, chunk):
        self.copy(owner, chunk, self.place.core_partner(), 0).wait_recv()

    def relay(self, chunk):
        owner = (self.place.mp + 2) % 4
        self.wait(owner, chunk)
        self.start(owner, chunk, self.place.core_partner(), 2)

    def rest(self):
        mp = self.place.mp
        other = mp + 1 - 2 * (mp % 2)
        for chunk in range(128 // CHUNK):
            self.wait(other, chunk)
        for chunk in range(128 // CHUNK):
            self.wait((other + 2) % 4, chunk)

    def finish(self):
        for copy in self.started:
            copy.wait_send()


ROWS_SEMS = [pltpu.SemaphoreType.DMA((3, 128 // CHUNK)), pltpu.SemaphoreType.DMA((4, 128 // CHUNK))]


def gather_kernel(normed, base, task, normed_all, base_all, task_all, *sems):
    place = Place()
    local = sems[6]
    copies = []
    for at, (source, target) in enumerate(((base, base_all), (task, task_all))):
        for kind in range(2):
            block = target.at[kind, pl.ds(pl.multiple_of(place.dp * 256, 256), 256), :]
            copies.append(pltpu.make_async_copy(source.at[kind], block, local.at[at * 2 + kind]))
    rows = normed_all.at[pl.ds(pl.multiple_of(place.mp * 128, 128), 128), :]
    copies.append(pltpu.make_async_copy(normed, rows, local.at[4]))
    for copy in copies:
        copy.start()
    greet(ring_devices(place) + [place.core_partner(), place.pair_chip()])
    for copy in copies:
        copy.wait()
    base_gather = Gather(place, base_all, sems[0], sems[1])
    task_gather = Gather(place, task_all, sems[2], sems[3])
    exchange = Rows(place, normed_all, sems[4], sems[5])
    base_gather.first()
    for chunk in range(128 // CHUNK):
        exchange.own(chunk)
    relays = list(range(128 // CHUNK))
    for at, (_, _, event) in enumerate(base_gather.events()):
        event()
        if at % 8 == 7 and relays:
            exchange.relay(relays.pop(0))
    task_gather.first()
    for at, (_, _, event) in enumerate(task_gather.events()):
        event()
        if relays:
            exchange.relay(relays.pop(0))
    exchange.rest()
    base_gather.finish()
    task_gather.finish()
    exchange.finish()


def gather_all(normed, base, task):
    any_spec = pl.BlockSpec(memory_space=pl.ANY)
    return pl.pallas_call(
        gather_kernel,
        out_shape=(
            jax.ShapeDtypeStruct((512, 8192), jnp.bfloat16),
            jax.ShapeDtypeStruct((2, 8192, 256), jnp.bfloat16),
            jax.ShapeDtypeStruct((2, 8192, 256), jnp.bfloat16),
        ),
        in_specs=[any_spec] * 3,
        out_specs=(any_spec,) * 3,
        scratch_shapes=GATHER_SEMS + GATHER_SEMS + ROWS_SEMS + [pltpu.SemaphoreType.DMA((5,))],
        compiler_params=pltpu.CompilerParams(collective_id=0, has_side_effects=True),
        name="gather_all",
    )(normed, base, task)


class Scatter:
    def __init__(self, place, part, land, send, recv):
        self.place, self.part, self.land, self.send, self.recv = place, part, land, send, recv
        self.slots = [0, 0]
        self.started = []

    def own(self, kind, along, across, half):
        return self.part.at[self.place.index(kind, along, across, half), kind]

    def copy(self, kind, block, spot, device, slot):
        return pltpu.make_async_remote_copy(
            src_ref=block,
            dst_ref=self.land.at[kind, spot],
            send_sem=self.send.at[kind, slot],
            recv_sem=self.recv.at[kind, spot],
            device_id=device,
            device_id_type=MESH,
        )

    def start(self, kind, block, spot, device):
        slot = self.slots[kind]
        self.slots[kind] += 1
        copy = self.copy(kind, block, spot, device, slot)
        copy.start()
        self.started.append(copy)

    def wait(self, kind, spot):
        block = self.land.at[kind, spot]
        self.copy(kind, block, spot, self.place.partner(), 0).wait_recv()

    def add(self, kind, block, spots):
        for spot in spots:
            self.wait(kind, spot)

        def step(at, carry):
            rows = pl.ds(pl.multiple_of(at * 64, 64), 64)
            total = block[rows, :].astype(jnp.float32)
            for spot in spots:
                total = total + self.land[kind, spot, rows, :].astype(jnp.float32)
            block[rows, :] = total.astype(jnp.bfloat16)
            return carry

        lax.fori_loop(0, 4, step, 0)

    def first(self, kind):
        for across in (2, 1, 3, 0):
            for half, along in ((0, 1), (1, -1)):
                block = self.own(kind, 2, across, half)
                self.start(kind, block, half * 4 + across, self.place.device(kind, along, 0))

    def second_own(self, kind):
        for across in (2, 1, 3, 0):
            for side, along in ((0, 1), (1, -1)):
                half = 1 - side
                block = self.own(kind, along, across, half)
                spot = 8 + side * 8 + across * 2 + half
                self.start(kind, block, spot, self.place.device(kind, along, 0))

    def second(self, kind, across):
        for side, along in ((0, 1), (1, -1)):
            half = side
            block = self.own(kind, along, across, half)
            self.add(kind, block, [side * 4 + across])
            spot = 8 + side * 8 + across * 2 + half
            self.start(kind, block, spot, self.place.device(kind, along, 0))

    def third(self, kind, across):
        for half in range(2):
            block = self.own(kind, 0, across, half)
            self.add(kind, block, [8 + across * 2 + half, 16 + across * 2 + half])
            if across == 2:
                along = 1 if half == 0 else -1
                self.start(kind, block, 24 + half, self.place.device(kind, 0, along))
            if across in (1, 3):
                side = 0 if across == 1 else 1
                if half != side:
                    along = 1 if side == 0 else -1
                    self.start(kind, block, 26 + side * 2 + half, self.place.device(kind, 0, along))

    def fourth(self, kind):
        for side, across in ((0, 1), (1, 3)):
            block = self.own(kind, 0, across, side)
            self.add(kind, block, [24 + side])
            along = 1 if side == 0 else -1
            self.start(kind, block, 26 + side * 2 + side, self.place.device(kind, 0, along))

    def fifth(self, kind):
        for half in (1 - self.place.h, self.place.h):
            block = self.own(kind, 0, 0, half)
            for side in range(2):
                self.wait(kind, 26 + side * 2 + half)

            def step(at, carry, block=block, half=half):
                rows = pl.ds(pl.multiple_of(at * 64, 64), 64)
                total = block[rows, :].astype(jnp.float32)
                for side in range(2):
                    total = total + self.land[kind, 26 + side * 2 + half, rows, :].astype(jnp.float32)
                block[rows, :] = total.astype(jnp.bfloat16)
                return carry

            lax.fori_loop(0, 4, step, 0)
            if half is not self.place.h:
                self.start(kind, block, 30, self.place.partner())

    def last(self, kind, grad):
        self.wait(kind, 30)
        block = self.own(kind, 0, 0, self.place.h)
        total = block[...].astype(jnp.float32) + self.land[kind, 30].astype(jnp.float32)
        grad[kind] = total.T

    def finish(self):
        for copy in self.started:
            copy.wait_send()


SCATTER_SCRATCH = [
    pltpu.VMEM((2, 31, 256, 256), jnp.bfloat16),
    pltpu.SemaphoreType.DMA((2, 31)),
    pltpu.SemaphoreType.DMA((2, 31)),
]


def scatter_kernel(given, grad, part, land, send, recv, local):
    place = Place()
    load = pltpu.make_async_copy(given, part, local)
    load.start()
    greet(ring_devices(place))
    load.wait()
    scatter = Scatter(place, part, land, send, recv)
    for kind in range(2):
        scatter.first(kind)
    for kind in range(2):
        scatter.second_own(kind)
    for across in (2, 1, 3, 0):
        for kind in range(2):
            scatter.second(kind, across)
    for across in (2, 1, 3, 0):
        for kind in range(2):
            scatter.third(kind, across)
    for kind in range(2):
        scatter.fourth(kind)
    for kind in range(2):
        scatter.fifth(kind)
    for kind in range(2):
        scatter.last(kind, grad)
    scatter.finish()


def scatter_all(part):
    return pl.pallas_call(
        scatter_kernel,
        out_shape=jax.ShapeDtypeStruct((2, 256, 256), jnp.float32),
        in_specs=[pl.BlockSpec(memory_space=pl.ANY)],
        out_specs=pl.BlockSpec(memory_space=pltpu.VMEM),
        scratch_shapes=[pltpu.VMEM((32, 2, 256, 256), jnp.bfloat16)] + SCATTER_SCRATCH + [pltpu.SemaphoreType.DMA],
        compiler_params=pltpu.CompilerParams(
            collective_id=1, has_side_effects=True, vmem_limit_bytes=40 * 1024 * 1024
        ),
        name="scatter_all",
    )(part)


def rotate(field, sign):
    length = field.shape[0]
    width = field.shape[-1]
    half_width = width // 2
    position = jnp.arange(length).astype(jnp.float32)
    frequency = jnp.power(1000000.0, -2.0 * jnp.arange(half_width).astype(jnp.float32) / width)
    angle = position[:, None] * frequency[None, :]
    angle = jnp.concatenate([angle, angle], axis=-1)
    cosine = jnp.cos(angle)[:, None, :]
    sine = sign * jnp.sin(angle)[:, None, :]
    turned = jnp.concatenate([-field[..., half_width:], field[..., :half_width]], axis=-1)
    return field * cosine + turned * sine


def multiply(form, left, right):
    return jnp.einsum(form, left, right, preferred_element_type=jnp.float32)


def attend(queries, query_tangent, cotangent, keys, values, key_tangent, value_tangent):
    factor = HEAD ** (-0.5)
    length = queries.shape[0]
    causal = jnp.arange(length)[:, None] >= jnp.arange(length)[None, :]
    scores = multiply("tkgh,skh->kgts", queries, keys) * factor
    scores = jnp.where(causal, scores, -jnp.inf)
    highest = jnp.max(scores, axis=-1, keepdims=True)
    raised = jnp.exp(scores - highest)
    weights = raised / jnp.sum(raised, axis=-1, keepdims=True)
    weights16 = weights.astype(jnp.bfloat16)
    context = multiply("kgts,skh->tkgh", weights16, values)
    spread = (
        multiply("tkgh,skh->kgts", query_tangent, keys)
        + multiply("tkgh,skh->kgts", queries, key_tangent)
    ) * factor
    moved = weights * (spread - jnp.sum(weights * spread, axis=-1, keepdims=True))
    moved16 = moved.astype(jnp.bfloat16)
    context_tangent = multiply("kgts,skh->tkgh", moved16, values) + multiply(
        "kgts,skh->tkgh", weights16, value_tangent
    )
    value_back = multiply("kgts,tkgh->skh", weights16, cotangent)
    pulled = multiply("tkgh,skh->kgts", cotangent, values)
    score_back = (
        weights * (pulled - jnp.sum(weights * pulled, axis=-1, keepdims=True)) * factor
    ).astype(jnp.bfloat16)
    key_turned = multiply("kgts,tkgh->skh", score_back, queries)
    return (context, context_tangent, key_turned, value_back)


def body(tokens, gain, query, query_tangent, kv_weight, kv_bias, kv_task, kv_bias_task, cotangent):
    wide = tokens.astype(jnp.float32)
    normed = (
        wide * lax.rsqrt(jnp.mean(wide * wide, axis=-1, keepdims=True) + 1e-06) * gain
    ).astype(jnp.bfloat16)
    normed_all, base_rows, task_rows = gather_all(normed, kv_weight, kv_task)
    length = normed_all.shape[0]
    local_width = kv_weight.shape[2]
    local_heads = local_width // HEAD

    def add_rows(weight_rows):
        return multiply("td,kdc->ktc", normed_all, weight_rows)

    base_kv = add_rows(base_rows)
    task_kv = add_rows(task_rows)
    base_kv = base_kv + kv_bias[:, None, :]
    task_kv = task_kv + kv_bias_task[:, None, :]
    heads_shape = (length, local_heads, HEAD)
    keys = rotate(base_kv[0].reshape(heads_shape), 1.0).astype(jnp.bfloat16)
    values = base_kv[1].reshape(heads_shape).astype(jnp.bfloat16)
    key_tangent = rotate(task_kv[0].reshape(heads_shape), 1.0).astype(jnp.bfloat16)
    value_tangent = task_kv[1].reshape(heads_shape).astype(jnp.bfloat16)
    grouped = (length, local_heads, -1, HEAD)
    queries = query.reshape(grouped)
    tangents = query_tangent.reshape(grouped)
    cotangents = cotangent.reshape(grouped)
    results = []
    for head_index in range(local_heads):
        pick = slice(head_index, head_index + 1)
        results.append(
            attend(
                queries[:, pick],
                tangents[:, pick],
                cotangents[:, pick],
                keys[:, pick],
                values[:, pick],
                key_tangent[:, pick],
                value_tangent[:, pick],
            )
        )
    context = (
        jnp.concatenate([item[0] for item in results], axis=1)
        .reshape(length, -1)
        .astype(jnp.bfloat16)
    )
    context_tangent = (
        jnp.concatenate([item[1] for item in results], axis=1)
        .reshape(length, -1)
        .astype(jnp.bfloat16)
    )
    key_turned = jnp.concatenate([item[2] for item in results], axis=1)
    value_back = jnp.concatenate([item[3] for item in results], axis=1).reshape(length, local_width)
    key_back = rotate(key_turned, -1.0).reshape(length, local_width)
    back16 = jnp.stack([key_back, value_back]).astype(jnp.bfloat16)
    part = multiply("ktc,td->kcd", back16, normed_all).astype(jnp.bfloat16)
    part = part.reshape(2, local_width, 32, 256).transpose(2, 0, 1, 3)
    kv_grad = scatter_all(part)
    unit_column = jnp.ones((length,), jnp.bfloat16)
    kv_bias_grad = lax.psum(multiply("t,ktc->kc", unit_column, back16), "dp")
    return (context, context_tangent, kv_grad, kv_bias_grad)


def solution(mesh):
    in_specs = (
        P(("dp", "mp"), None),
        P(),
        P("dp", "mp"),
        P("dp", "mp"),
        P(None, "dp", "mp"),
        P(None, "mp"),
        P(None, "dp", "mp"),
        P(None, "mp"),
        P("dp", "mp"),
    )
    out_specs = (P("dp", "mp"), P("dp", "mp"), P(None, "dp", "mp"), P(None, "mp"))
    return jax.shard_map(body, mesh=mesh, in_specs=in_specs, out_specs=out_specs, check_vma=False)
```

```python
import functools

import jax
import jax.numpy as jnp
import numpy as np
from jax import lax
from jax.experimental import pallas as pl
from jax.experimental.pallas import tpu as pltpu
from jax.sharding import PartitionSpec as P

HEAD = 128
MESH = pl.DeviceIdType.MESH


class Place:
    def __init__(self):
        dp = lax.axis_index("dp")
        self.mp = lax.axis_index("mp")
        self.z, self.y, self.h = dp // 8, (dp // 2) % 4, dp % 2
        self.dp = dp

    def index(self, kind, along, across, half):
        dy, dz = (along, across) if kind == 0 else (across, along)
        return ((self.z + dz + 4) % 4) * 8 + ((self.y + dy + 4) % 4) * 2 + half

    def device(self, kind, along, across):
        return (self.index(kind, along, across, self.h), self.mp)

    def partner(self):
        return (self.dp + 1 - 2 * self.h, self.mp)

    def core_partner(self):
        return (self.dp, self.mp + 1 - 2 * (self.mp % 2))

    def pair_chip(self):
        return (self.dp, (self.mp + 2) % 4)


def greet(devices):
    barrier = pltpu.get_barrier_semaphore()
    for device in devices:
        pl.semaphore_signal(barrier, inc=1, device_id=device, device_id_type=MESH)
    pl.semaphore_wait(barrier, len(devices))


def ring_devices(place):
    return [
        place.device(0, 1, 0),
        place.device(0, -1, 0),
        place.device(0, 0, 1),
        place.device(0, 0, -1),
        place.partner(),
    ]


class Gather:
    def __init__(self, place, whole, send, recv):
        self.place, self.whole, self.send, self.recv = place, whole, send, recv
        self.slots = [0, 0]
        self.started = []

    def shard(self, kind, index):
        return self.whole.at[kind, index]

    def copy(self, kind, index, device, slot):
        block = self.shard(kind, index)
        return pltpu.make_async_remote_copy(
            src_ref=block,
            dst_ref=block,
            send_sem=self.send.at[kind, slot],
            recv_sem=self.recv.at[kind, index],
            device_id=device,
            device_id_type=MESH,
        )

    def start(self, kind, index, device):
        slot = self.slots[kind]
        self.slots[kind] += 1
        copy = self.copy(kind, index, device, slot)
        copy.start()
        self.started.append(copy)

    def wait(self, kind, index):
        self.copy(kind, index, self.place.partner(), 0).wait_recv()

    def spread(self, kind, index, along):
        if along:
            self.start(kind, index, self.place.device(kind, 1, 0))
            self.start(kind, index, self.place.device(kind, -1, 0))
        self.start(kind, index, self.place.device(kind, 0, 1))
        self.start(kind, index, self.place.device(kind, 0, -1))

    def first(self):
        own = self.place.dp
        for kind in range(2):
            self.start(kind, own, self.place.partner())
        for kind in range(2):
            self.spread(kind, own, True)

    def events(self):
        place = self.place

        def partner(kind):
            other = place.index(kind, 0, 0, 1 - place.h)
            self.wait(kind, other)
            self.spread(kind, other, True)

        def side(kind, along):
            near, far = (0, 1) if along < 0 else (1, 0)
            index = place.index(kind, along, 0, near)
            self.wait(kind, index)
            self.start(kind, index, place.device(kind, -along, 0))
            self.spread(kind, index, False)
            index = place.index(kind, along, 0, far)
            self.wait(kind, index)
            self.spread(kind, index, False)

        def opposite(kind):
            for half in range(2):
                index = place.index(kind, 2, 0, half)
                self.wait(kind, index)
                self.spread(kind, index, False)

        def across(kind, along, step):
            near, far = (0, 1) if step < 0 else (1, 0)
            index = place.index(kind, along, step, near)
            self.wait(kind, index)
            self.start(kind, index, place.device(kind, 0, -step))
            self.wait(kind, place.index(kind, along, step, far))

        def across_opposite(kind, along):
            for half in range(2):
                self.wait(kind, place.index(kind, along, 2, half))

        result = []

        def add(blocks, function, *rest):
            for kind in range(2):
                result.append((kind, blocks, functools.partial(function, kind, *rest)))

        add([(0, 0)], partner)
        add([(-1, 0)], side, -1)
        add([(1, 0)], side, 1)
        add([(0, -1)], across, 0, -1)
        add([(0, 1)], across, 0, 1)
        add([(2, 0)], opposite)
        for along in (-1, 1, 2):
            add([(along, -1)], across, along, -1)
            add([(along, 1)], across, along, 1)
            before = {-1: 0, 1: -1, 2: 1}[along]
            add([(before, 2)], across_opposite, before)
        add([(2, 2)], across_opposite, 2)
        return result

    def finish(self):
        for copy in self.started:
            copy.wait_send()


GATHER_SEMS = [pltpu.SemaphoreType.DMA((2, 31)), pltpu.SemaphoreType.DMA((2, 32))]
CHUNK = 32


class Rows:
    def __init__(self, place, whole, send, recv):
        self.place, self.whole, self.send, self.recv = place, whole, send, recv
        self.started = []

    def copy(self, owner, chunk, device, lane):
        rows = pl.multiple_of(owner * 128 + chunk * CHUNK, CHUNK)
        block = self.whole.at[pl.ds(rows, CHUNK), :]
        return pltpu.make_async_remote_copy(
            src_ref=block,
            dst_ref=block,
            send_sem=self.send.at[lane, chunk],
            recv_sem=self.recv.at[owner, chunk],
            device_id=device,
            device_id_type=MESH,
        )

    def start(self, owner, chunk, device, lane):
        copy = self.copy(owner, chunk, device, lane)
        copy.start()
        self.started.append(copy)

    def own(self, chunk):
        self.start(self.place.mp, chunk, self.place.pair_chip(), 0)
        self.start(self.place.mp, chunk, self.place.core_partner(), 1)

    def wait(self, owner, chunk):
        self.copy(owner, chunk, self.place.core_partner(), 0).wait_recv()

    def relay(self, chunk):
        owner = (self.place.mp + 2) % 4
        self.wait(owner, chunk)
        self.start(owner, chunk, self.place.core_partner(), 2)

    def rest(self):
        mp = self.place.mp
        other = mp + 1 - 2 * (mp % 2)
        for chunk in range(128 // CHUNK):
            self.wait(other, chunk)
        for chunk in range(128 // CHUNK):
            self.wait((other + 2) % 4, chunk)

    def finish(self):
        for copy in self.started:
            copy.wait_send()


ROWS_SEMS = [pltpu.SemaphoreType.DMA((3, 128 // CHUNK)), pltpu.SemaphoreType.DMA((4, 128 // CHUNK))]


class Scatter:
    def __init__(self, place, part, land, send, recv):
        self.place, self.part, self.land, self.send, self.recv = place, part, land, send, recv
        self.slots = [0, 0]
        self.started = []

    def own(self, kind, along, across, half):
        return self.part.at[kind, self.place.index(kind, along, across, half)]

    def copy(self, kind, block, spot, device, slot):
        return pltpu.make_async_remote_copy(
            src_ref=block,
            dst_ref=self.land.at[kind, spot],
            send_sem=self.send.at[kind, slot],
            recv_sem=self.recv.at[kind, spot],
            device_id=device,
            device_id_type=MESH,
        )

    def start(self, kind, block, spot, device):
        slot = self.slots[kind]
        self.slots[kind] += 1
        copy = self.copy(kind, block, spot, device, slot)
        copy.start()
        self.started.append(copy)

    def wait(self, kind, spot):
        block = self.land.at[kind, spot]
        self.copy(kind, block, spot, self.place.partner(), 0).wait_recv()

    def add(self, kind, block, spots):
        for spot in spots:
            self.wait(kind, spot)

        def step(at, carry):
            rows = pl.ds(pl.multiple_of(at * 64, 64), 64)
            total = block[rows, :].astype(jnp.float32)
            for spot in spots:
                total = total + self.land[kind, spot, rows, :].astype(jnp.float32)
            block[rows, :] = total.astype(jnp.bfloat16)
            return carry

        lax.fori_loop(0, 4, step, 0)

    def first(self, kind):
        for across in (2, 1, 3, 0):
            for half, along in ((0, 1), (1, -1)):
                block = self.own(kind, 2, across, half)
                self.start(kind, block, half * 4 + across, self.place.device(kind, along, 0))

    def second_own(self, kind):
        for across in (2, 1, 3, 0):
            for side, along in ((0, 1), (1, -1)):
                half = 1 - side
                block = self.own(kind, along, across, half)
                spot = 8 + side * 8 + across * 2 + half
                self.start(kind, block, spot, self.place.device(kind, along, 0))

    def second(self, kind, across):
        for side, along in ((0, 1), (1, -1)):
            half = side
            block = self.own(kind, along, across, half)
            self.add(kind, block, [side * 4 + across])
            spot = 8 + side * 8 + across * 2 + half
            self.start(kind, block, spot, self.place.device(kind, along, 0))

    def third(self, kind, across):
        for half in range(2):
            block = self.own(kind, 0, across, half)
            self.add(kind, block, [8 + across * 2 + half, 16 + across * 2 + half])
            if across == 2:
                along = 1 if half == 0 else -1
                self.start(kind, block, 24 + half, self.place.device(kind, 0, along))
            if across in (1, 3):
                side = 0 if across == 1 else 1
                if half != side:
                    along = 1 if side == 0 else -1
                    self.start(kind, block, 26 + side * 2 + half, self.place.device(kind, 0, along))

    def fourth(self, kind):
        for side, across in ((0, 1), (1, 3)):
            block = self.own(kind, 0, across, side)
            self.add(kind, block, [24 + side])
            along = 1 if side == 0 else -1
            self.start(kind, block, 26 + side * 2 + side, self.place.device(kind, 0, along))

    def fifth(self, kind):
        for half in (1 - self.place.h, self.place.h):
            block = self.own(kind, 0, 0, half)
            for side in range(2):
                self.wait(kind, 26 + side * 2 + half)

            def step(at, carry, block=block, half=half):
                rows = pl.ds(pl.multiple_of(at * 64, 64), 64)
                total = block[rows, :].astype(jnp.float32)
                for side in range(2):
                    total = total + self.land[kind, 26 + side * 2 + half, rows, :].astype(jnp.float32)
                block[rows, :] = total.astype(jnp.bfloat16)
                return carry

            lax.fori_loop(0, 4, step, 0)
            if half is not self.place.h:
                self.start(kind, block, 30, self.place.partner())

    def last(self, kind, grad):
        self.wait(kind, 30)
        block = self.own(kind, 0, 0, self.place.h)
        total = block[...].astype(jnp.float32) + self.land[kind, 30].astype(jnp.float32)
        grad[kind] = total.T

    def finish(self):
        for copy in self.started:
            copy.wait_send()


FACTOR = HEAD ** (-0.5)
EXPONENT = FACTOR * 1.4426950408889634
F32 = jnp.float32
BF16 = jnp.bfloat16


def product(left, right):
    return jnp.dot(left, right, preferred_element_type=F32)


def product_rows(left, right):
    return lax.dot_general(left, right, (((1,), (1,)), ((), ())), preferred_element_type=F32)


def turn(field, cosine, sine):
    parts = []
    for head in range(2):
        one = field[:, head * HEAD : (head + 1) * HEAD]
        parts.append(one * cosine + pltpu.roll(one, HEAD // 2, 1) * sine)
    return jnp.concatenate(parts, axis=1)


def softmax_down(keys, queries):
    scores = product_rows(keys, queries)
    ahead = lax.broadcasted_iota(jnp.int32, (256, 256), 0) > lax.broadcasted_iota(jnp.int32, (256, 256), 1)
    own = jnp.where(ahead, -jnp.inf, scores[-256:])
    scores = own if scores.shape[0] == 256 else jnp.concatenate([scores[:-256], own], axis=0)
    highest = jnp.max(scores, axis=0, keepdims=True)
    raised = jnp.exp2((scores - highest) * EXPONENT)
    return raised * (1.0 / jnp.sum(raised, axis=0, keepdims=True))


def columns(head):
    return pl.ds(pl.multiple_of(head * HEAD, HEAD), HEAD)


def base_head(head, query, cotangent, keys, values, key_sum, value_sum):
    group = head // 8
    for block in range(2):
        rows, count = pl.ds(block * 256, 256), (block + 1) * 256
        queries, pulls = query[rows, columns(head)], cotangent[rows, columns(head)]
        weights = softmax_down(keys[:count, columns(group)], queries)
        pulled = product_rows(values[:count, columns(group)], pulls)
        mean = jnp.sum(weights * pulled, axis=0, keepdims=True)
        back = (weights * (pulled - mean) * FACTOR).astype(BF16)
        value_sum[:count, columns(group)] += product(weights.astype(BF16), pulls)
        key_sum[:count, columns(group)] += product(back, queries)


def tangent_head(head, query, tangent, keys, key_tangent, turned, context, context_tangent):
    group = head // 8
    for block in range(2):
        rows, count = pl.ds(block * 256, 256), (block + 1) * 256
        queries = query[rows, columns(head)]
        weights = softmax_down(keys[:count, columns(group)], queries)
        both_keys = jnp.concatenate([keys[:count, columns(group)], key_tangent[:count, columns(group)]], axis=1)
        both_queries = jnp.concatenate([tangent[rows, columns(head)], queries], axis=1)
        spread = product_rows(both_keys, both_queries)
        mean = jnp.sum(weights * spread, axis=0, keepdims=True)
        moved = (weights * (spread - mean) * FACTOR).astype(BF16)
        first = product(turned[group, :, :count], weights.astype(BF16))
        second = product(turned[group, :HEAD, :count], moved)
        context[rows, columns(head)] = first[:HEAD].T.astype(BF16)
        context_tangent[rows, columns(head)] = (first[HEAD:] + second).T.astype(BF16)


def project(normed, whole, bias, total):
    total[...] = jnp.zeros_like(total) + jnp.concatenate([bias[0:1, :], bias[1:2, :]], axis=1)

    def step(at, carry):
        for kind in range(2):
            sums = 0.0
            for part in range(4):
                index = at * 4 + part
                left = normed[:, pl.ds(pl.multiple_of(index * 256, 256), 256)]
                sums = sums + product(left, whole[kind, index])
            total[:, kind * 256 : (kind + 1) * 256] += sums
        return carry

    lax.fori_loop(0, 8, step, 0)


def layer_kernel(
    tokens, gain, query_in, tangent_in, kv_in, bias, task_in, bias_task, cotangent_in, cosine, sine,
    context, context_tangent, grad, bias_grad,
    token_rows, query, tangent, cotangent, normed, base_all, task_all, land, total,
    keys, values, key_tangent, value_tangent, turned, key_sum, value_sum, back, sums, sums_land,
    local, base_send, base_recv, task_send, task_recv, rows_send, rows_recv,
    part_send, part_recv, sums_send, sums_recv,
):
    place = Place()

    def load(source, target, at):
        copy = pltpu.make_async_copy(source, target, local.at[at])
        copy.start()
        return copy

    waits = []
    for kind in range(2):
        waits.append(load(kv_in.at[kind], base_all.at[kind, place.dp], kind))
        waits.append(load(task_in.at[kind], task_all.at[kind, place.dp], 2 + kind))
    waits.append(load(tokens, token_rows, 4))
    later = [load(query_in, query, 5), load(cotangent_in, cotangent, 6), load(tangent_in, tangent, 7)]
    greet(ring_devices(place) + [place.core_partner(), place.pair_chip()])
    for copy in waits:
        copy.wait()
    base = Gather(place, base_all, base_send, base_recv)
    task = Gather(place, task_all, task_send, task_recv)
    rows = Rows(place, normed, rows_send, rows_recv)
    base.first()

    scale = gain[...]
    for chunk in range(128 // CHUNK):

        def norm(at, carry, chunk=chunk):
            here = pl.multiple_of(chunk * CHUNK + at * 16, 16)
            wide = token_rows[pl.ds(here, 16), :].astype(F32)
            mean = jnp.mean(wide * wide, axis=-1, keepdims=True)
            there = pl.multiple_of(place.mp * 128 + here, 16)
            normed[pl.ds(there, 16), :] = (wide * lax.rsqrt(mean + 1e-06) * scale).astype(BF16)
            return carry

        lax.fori_loop(0, CHUNK // 16, norm, 0)
        rows.own(chunk)
    for copy in later:
        copy.wait()

    relays = list(range(128 // CHUNK))
    for at, (_, _, event) in enumerate(base.events()):
        event()
        if at in (12, 18, 23):
            rows.relay(relays.pop(0))
    task.first()
    for chunk in relays:
        rows.relay(chunk)
    rows.rest()
    ahead = [event for _, _, event in task.events()]

    def events(count):
        for _ in range(min(count, len(ahead))):
            ahead.pop(0)()

    project(normed, base_all, bias, total)
    events(4)
    keys[...] = turn(total[:, :256], cosine[...], sine[...]).astype(BF16)
    values[...] = total[:, 256:].astype(BF16)
    key_sum[...] = jnp.zeros_like(key_sum)
    value_sum[...] = jnp.zeros_like(value_sum)
    for quarter in range(4):

        def base_step(at, carry, quarter=quarter):
            base_head(quarter * 4 + at, query, cotangent, keys, values, key_sum, value_sum)
            return carry

        lax.fori_loop(0, 4, base_step, 0)
        events(4)

    key_back = turn(key_sum[...], cosine[...], -sine[...]).astype(BF16)
    value_back = value_sum[...].astype(BF16)
    back[:256, :] = key_back.astype(F32).T.astype(BF16)
    back[256:, :] = value_back.astype(F32).T.astype(BF16)
    sums[0] = jnp.zeros_like(sums[0])
    sums[0, 0:1, :] = jnp.sum(key_back.astype(F32), axis=0, keepdims=True)
    sums[0, 1:2, :] = jnp.sum(value_back.astype(F32), axis=0, keepdims=True)
    base.finish()

    def grad_step(at, carry):
        block = product(back[...], normed[:, pl.ds(pl.multiple_of(at * 256, 256), 256)]).astype(BF16)
        base_all[0, at] = block[:256]
        base_all[1, at] = block[256:]
        return carry

    lax.fori_loop(0, 32, grad_step, 0)
    scatter = Scatter(place, base_all, land, part_send, part_recv)

    odd_y, odd_z = place.y % 2, place.z % 2
    mates = [
        place.device(0, 1 - 2 * odd_y, 0),
        place.device(0, 2 * odd_y - 1, 0),
        place.device(1, 1 - 2 * odd_z, 0),
        place.device(1, 2 * odd_z - 1, 0),
        place.partner(),
    ]

    def mate_copy(at):
        return pltpu.make_async_remote_copy(
            src_ref=sums.at[at],
            dst_ref=sums_land.at[at],
            send_sem=sums_send.at[at],
            recv_sem=sums_recv.at[at],
            device_id=mates[at],
            device_id_type=MESH,
        )

    def mate_sum(at):
        mate_copy(at).wait()
        sums[at + 1] = sums[at] + sums_land[at]
        if at + 1 < 5:
            mate_copy(at + 1).start()

    events(len(ahead))
    for kind in range(2):
        scatter.first(kind)
    for kind in range(2):
        scatter.second_own(kind)
    mate_copy(0).start()
    project(normed, task_all, bias_task, total)
    key_tangent[...] = turn(total[:, :256], cosine[...], sine[...]).astype(BF16)
    value_tangent[...] = total[:, 256:].astype(BF16)
    for group in range(2):
        pick = slice(group * HEAD, (group + 1) * HEAD)
        turned[group, :HEAD, :] = values[:, pick].astype(F32).T.astype(BF16)
        turned[group, HEAD:, :] = value_tangent[:, pick].astype(F32).T.astype(BF16)

    def tangents(start, count):
        def step(at, carry):
            tangent_head(start + at, query, tangent, keys, key_tangent, turned, context, context_tangent)
            return carry

        lax.fori_loop(0, count, step, 0)

    for at, across in enumerate((2, 1, 3, 0)):
        mate_sum(at)
        for kind in range(2):
            scatter.second(kind, across)
        if at % 2 == 1:
            tangents(at // 2 * 4, 4)
    mate_sum(4)
    for across in (2, 1, 3, 0):
        for kind in range(2):
            scatter.third(kind, across)
    tangents(8, 4)
    for kind in range(2):
        scatter.fourth(kind)
    tangents(12, 4)
    for kind in range(2):
        scatter.fifth(kind)
    for kind in range(2):
        scatter.last(kind, grad)
    bias_grad[...] = sums[5, 0:2, :]
    scatter.finish()
    task.finish()
    rows.finish()


def layer(*operands):
    vmem = pl.BlockSpec(memory_space=pltpu.VMEM)
    hbm = pl.BlockSpec(memory_space=pl.ANY)
    scratch = [
        pltpu.VMEM((128, 8192), BF16),
        pltpu.VMEM((512, 2048), BF16),
        pltpu.VMEM((512, 2048), BF16),
        pltpu.VMEM((512, 2048), BF16),
        pltpu.VMEM((512, 8192), BF16),
        pltpu.VMEM((2, 32, 256, 256), BF16),
        pltpu.VMEM((2, 32, 256, 256), BF16),
        pltpu.VMEM((2, 31, 256, 256), BF16),
        pltpu.VMEM((512, 512), F32),
        pltpu.VMEM((512, 256), BF16),
        pltpu.VMEM((512, 256), BF16),
        pltpu.VMEM((512, 256), BF16),
        pltpu.VMEM((512, 256), BF16),
        pltpu.VMEM((2, 256, 512), BF16),
        pltpu.VMEM((512, 256), F32),
        pltpu.VMEM((512, 256), F32),
        pltpu.VMEM((512, 512), BF16),
        pltpu.VMEM((6, 8, 256), F32),
        pltpu.VMEM((5, 8, 256), F32),
        pltpu.SemaphoreType.DMA((8,)),
        *GATHER_SEMS,
        *GATHER_SEMS,
        *ROWS_SEMS,
        pltpu.SemaphoreType.DMA((2, 31)),
        pltpu.SemaphoreType.DMA((2, 31)),
        pltpu.SemaphoreType.DMA((5,)),
        pltpu.SemaphoreType.DMA((5,)),
    ]
    return pl.pallas_call(
        layer_kernel,
        out_shape=(
            jax.ShapeDtypeStruct((512, 2048), BF16),
            jax.ShapeDtypeStruct((512, 2048), BF16),
            jax.ShapeDtypeStruct((2, 256, 256), F32),
            jax.ShapeDtypeStruct((2, 256), F32),
        ),
        in_specs=[hbm, vmem, hbm, hbm, hbm, vmem, hbm, vmem, hbm, vmem, vmem],
        out_specs=(vmem,) * 4,
        scratch_shapes=scratch,
        compiler_params=pltpu.CompilerParams(
            collective_id=0, has_side_effects=True, vmem_limit_bytes=62 * 1024 * 1024
        ),
        name="layer",
    )(*operands)


def turning_tables():
    position = np.arange(512, dtype=np.float64)[:, None]
    frequency = 1000000.0 ** (-2.0 * np.arange(64) / 128)
    angle = position * frequency[None, :]
    cosine, sine = np.cos(angle), np.sin(angle)
    return (
        np.concatenate([cosine, cosine], axis=1).astype(np.float32),
        np.concatenate([-sine, sine], axis=1).astype(np.float32),
    )


def body(tokens, gain, query, query_tangent, kv_weight, kv_bias, kv_task, kv_bias_task, cotangent):
    cosine, sine = turning_tables()
    return layer(
        tokens, gain.reshape(1, -1), query, query_tangent, kv_weight, kv_bias, kv_task, kv_bias_task, cotangent,
        jnp.asarray(cosine), jnp.asarray(sine),
    )


def solution(mesh):
    in_specs = (
        P(("dp", "mp"), None),
        P(),
        P("dp", "mp"),
        P("dp", "mp"),
        P(None, "dp", "mp"),
        P(None, "mp"),
        P(None, "dp", "mp"),
        P(None, "mp"),
        P("dp", "mp"),
    )
    out_specs = (P("dp", "mp"), P("dp", "mp"), P(None, "dp", "mp"), P(None, "mp"))
    return jax.shard_map(body, mesh=mesh, in_specs=in_specs, out_specs=out_specs, check_vma=False)
```

```python
import functools

import jax
import jax.numpy as jnp
import numpy as np
from jax import lax
from jax.experimental import pallas as pl
from jax.experimental.pallas import tpu as pltpu
from jax.sharding import PartitionSpec as P

HEAD = 128
MESH = pl.DeviceIdType.MESH


class Place:
    def __init__(self):
        dp = lax.axis_index("dp")
        self.mp = lax.axis_index("mp")
        self.z, self.y, self.h = dp // 8, (dp // 2) % 4, dp % 2
        self.dp = dp

    def index(self, kind, along, across, half):
        dy, dz = (along, across) if kind == 0 else (across, along)
        return ((self.z + dz + 4) % 4) * 8 + ((self.y + dy + 4) % 4) * 2 + half

    def device(self, kind, along, across):
        return (self.index(kind, along, across, self.h), self.mp)

    def partner(self):
        return (self.dp + 1 - 2 * self.h, self.mp)

    def core_partner(self):
        return (self.dp, self.mp + 1 - 2 * (self.mp % 2))

    def pair_chip(self):
        return (self.dp, (self.mp + 2) % 4)

    def other_block(self):
        x = (self.h * 2 + self.mp // 2 + 2 * (self.mp // 2) + 3) % 4
        return x * 2 + self.mp % 2

    def other_chip(self):
        block = self.other_block()
        return (self.dp - self.h + block // 4, block % 4)


def greet(devices):
    barrier = pltpu.get_barrier_semaphore()
    for device in devices:
        pl.semaphore_signal(barrier, inc=1, device_id=device, device_id_type=MESH)
    pl.semaphore_wait(barrier, len(devices))


def ring_devices(place):
    return [
        place.device(0, 1, 0),
        place.device(0, -1, 0),
        place.device(0, 0, 1),
        place.device(0, 0, -1),
        place.partner(),
    ]


class Gather:
    def __init__(self, place, piece, partner_piece, send, recv):
        self.place, self.piece, self.partner_piece = place, piece, partner_piece
        self.send, self.recv = send, recv
        self.slots = [0, 0]
        self.started = []

    def copy(self, kind, index, device, slot, source=None):
        block = self.piece(kind, index)
        return pltpu.make_async_remote_copy(
            src_ref=block if source is None else source,
            dst_ref=block,
            send_sem=self.send.at[kind, slot],
            recv_sem=self.recv.at[kind, index],
            device_id=device,
            device_id_type=MESH,
        )

    def start(self, kind, index, device, source=None):
        slot = self.slots[kind]
        self.slots[kind] += 1
        copy = self.copy(kind, index, device, slot, source)
        copy.start()
        self.started.append(copy)

    def wait(self, kind, index):
        self.copy(kind, index, self.place.partner(), 0).wait_recv()

    def spread(self, kind, index, along):
        if along:
            self.start(kind, index, self.place.device(kind, 1, 0))
            self.start(kind, index, self.place.device(kind, -1, 0))
        self.start(kind, index, self.place.device(kind, 0, 1))
        self.start(kind, index, self.place.device(kind, 0, -1))

    def first(self):
        own = self.place.dp
        for kind in range(2):
            self.start(kind, own, self.place.partner(), self.partner_piece(kind))
        for kind in range(2):
            self.spread(kind, own, True)

    def events(self):
        place = self.place

        def partner(kind):
            other = place.index(kind, 0, 0, 1 - place.h)
            self.wait(kind, other)
            self.spread(kind, other, True)

        def side(kind, along):
            near, far = (0, 1) if along < 0 else (1, 0)
            index = place.index(kind, along, 0, near)
            self.wait(kind, index)
            self.start(kind, index, place.device(kind, -along, 0))
            self.spread(kind, index, False)
            index = place.index(kind, along, 0, far)
            self.wait(kind, index)
            self.spread(kind, index, False)

        def opposite(kind):
            for half in range(2):
                index = place.index(kind, 2, 0, half)
                self.wait(kind, index)
                self.spread(kind, index, False)

        def across(kind, along, step):
            near, far = (0, 1) if step < 0 else (1, 0)
            index = place.index(kind, along, step, near)
            self.wait(kind, index)
            self.start(kind, index, place.device(kind, 0, -step))
            self.wait(kind, place.index(kind, along, step, far))

        def across_opposite(kind, along):
            for half in range(2):
                self.wait(kind, place.index(kind, along, 2, half))

        result = []

        def add(blocks, function, *rest):
            for kind in range(2):
                result.append((kind, blocks, functools.partial(function, kind, *rest)))

        add([(0, 0)], partner)
        add([(-1, 0)], side, -1)
        add([(1, 0)], side, 1)
        add([(0, -1)], across, 0, -1)
        add([(0, 1)], across, 0, 1)
        add([(2, 0)], opposite)
        for along in (-1, 1, 2):
            add([(along, -1)], across, along, -1)
            add([(along, 1)], across, along, 1)
            before = {-1: 0, 1: -1, 2: 1}[along]
            add([(before, 2)], across_opposite, before)
        add([(2, 2)], across_opposite, 2)
        return result

    def finish(self):
        for copy in self.started:
            copy.wait_send()


GATHER_SEMS = [pltpu.SemaphoreType.DMA((2, 31)), pltpu.SemaphoreType.DMA((2, 32))]
CHUNK = 32


class Rows:
    def __init__(self, place, whole, send, recv):
        self.place, self.whole, self.send, self.recv = place, whole, send, recv
        mp, h = place.mp, place.h
        self.mine = h * 4 + mp
        self.pair = h * 4 + (mp + 2) % 4
        self.other = place.other_block()
        x = (h * 2 + mp // 2 + 2) % 4
        self.far = x * 2 + mp % 2
        self.started = []

    def copy(self, owner, chunk, device, lane):
        rows = pl.multiple_of(owner * 128 + chunk * CHUNK, CHUNK)
        block = self.whole.at[pl.ds(rows, CHUNK), :]
        return pltpu.make_async_remote_copy(
            src_ref=block,
            dst_ref=block,
            send_sem=self.send.at[lane, chunk],
            recv_sem=self.recv.at[owner, chunk],
            device_id=device,
            device_id_type=MESH,
        )

    def start(self, owner, chunk, device, lane):
        copy = self.copy(owner, chunk, device, lane)
        copy.start()
        self.started.append(copy)

    def own(self, chunk):
        self.start(self.mine, chunk, self.place.pair_chip(), 0)
        self.start(self.mine, chunk, self.place.other_chip(), 1)
        self.start(self.mine, chunk, self.place.core_partner(), 2)

    def wait(self, owner, chunk):
        self.copy(owner, chunk, self.place.core_partner(), 0).wait_recv()

    def arrive(self, chunk):
        for owner, lane in ((self.pair, 3), (self.other, 4)):
            self.wait(owner, chunk)
            self.start(owner, chunk, self.place.core_partner(), lane)

    def relay(self, chunk):
        if chunk < 128 // CHUNK // 2:
            self.start(self.pair, chunk, self.place.other_chip(), 5)
        else:
            self.start(self.other, chunk, self.place.pair_chip(), 5)

    def arrive_far(self, chunk):
        self.wait(self.far, chunk)
        self.start(self.far, chunk, self.place.core_partner(), 6)

    def rest(self, owners):
        for owner in owners:
            for chunk in range(128 // CHUNK):
                self.wait(owner + 1 - 2 * (owner % 2), chunk)

    def finish(self):
        for copy in self.started:
            copy.wait_send()


ROWS_SEMS = [pltpu.SemaphoreType.DMA((7, 128 // CHUNK)), pltpu.SemaphoreType.DMA((8, 128 // CHUNK))]


class Scatter:
    def __init__(self, place, part, land, send, recv):
        self.place, self.part, self.land, self.send, self.recv = place, part, land, send, recv
        self.slots = [0, 0]
        self.started = []

    def own(self, kind, along, across, half):
        return self.part.at[self.place.index(kind, along, across, half), pl.ds(kind * 128, 128), :]

    def copy(self, kind, block, spot, device, slot):
        return pltpu.make_async_remote_copy(
            src_ref=block,
            dst_ref=self.land.at[kind, spot],
            send_sem=self.send.at[kind, slot],
            recv_sem=self.recv.at[kind, spot],
            device_id=device,
            device_id_type=MESH,
        )

    def start(self, kind, block, spot, device):
        slot = self.slots[kind]
        self.slots[kind] += 1
        copy = self.copy(kind, block, spot, device, slot)
        copy.start()
        self.started.append(copy)

    def wait(self, kind, spot):
        block = self.land.at[kind, spot]
        self.copy(kind, block, spot, self.place.partner(), 0).wait_recv()

    def add(self, kind, block, spots):
        for spot in spots:
            self.wait(kind, spot)

        def step(at, carry):
            rows = pl.ds(pl.multiple_of(at * 64, 64), 64)
            total = block[rows, :].astype(jnp.float32)
            for spot in spots:
                total = total + self.land[kind, spot, rows, :].astype(jnp.float32)
            block[rows, :] = total.astype(jnp.bfloat16)
            return carry

        lax.fori_loop(0, 2, step, 0)

    def first(self, kind):
        for across in (2, 1, 3, 0):
            for half, along in ((0, 1), (1, -1)):
                block = self.own(kind, 2, across, half)
                self.start(kind, block, half * 4 + across, self.place.device(kind, along, 0))

    def second_own(self, kind):
        for across in (2, 1, 3, 0):
            for side, along in ((0, 1), (1, -1)):
                half = 1 - side
                block = self.own(kind, along, across, half)
                spot = 8 + side * 8 + across * 2 + half
                self.start(kind, block, spot, self.place.device(kind, along, 0))

    def second(self, kind, across):
        for side, along in ((0, 1), (1, -1)):
            half = side
            block = self.own(kind, along, across, half)
            self.add(kind, block, [side * 4 + across])
            spot = 8 + side * 8 + across * 2 + half
            self.start(kind, block, spot, self.place.device(kind, along, 0))

    def third(self, kind, across):
        for half in range(2):
            block = self.own(kind, 0, across, half)
            self.add(kind, block, [8 + across * 2 + half, 16 + across * 2 + half])
            if across == 2:
                along = 1 if half == 0 else -1
                self.start(kind, block, 24 + half, self.place.device(kind, 0, along))
            if across in (1, 3):
                side = 0 if across == 1 else 1
                if half != side:
                    along = 1 if side == 0 else -1
                    self.start(kind, block, 26 + side * 2 + half, self.place.device(kind, 0, along))

    def fourth(self, kind):
        for side, across in ((0, 1), (1, 3)):
            block = self.own(kind, 0, across, side)
            self.add(kind, block, [24 + side])
            along = 1 if side == 0 else -1
            self.start(kind, block, 26 + side * 2 + side, self.place.device(kind, 0, along))

    def fifth(self, kind, grad):
        for half in (1 - self.place.h, self.place.h):
            for side in range(2):
                self.wait(kind, 26 + side * 2 + half)
        block = self.own(kind, 0, 0, 1 - self.place.h)
        block[...] = self.summed(kind, 1 - self.place.h).astype(jnp.bfloat16)
        self.start(kind, block, 30, self.place.partner())
        grad[self.place.h, :, kind * 128 : (kind + 1) * 128] = self.summed(kind, self.place.h).T

    def summed(self, kind, half):
        total = self.own(kind, 0, 0, half)[...].astype(jnp.float32)
        for side in range(2):
            total = total + self.land[kind, 26 + side * 2 + half].astype(jnp.float32)
        return total

    def last(self, kind, grad):
        self.wait(kind, 30)
        block = self.land[kind, 30].astype(jnp.float32)
        grad[1 - self.place.h, :, kind * 128 : (kind + 1) * 128] = block.T

    def finish(self):
        for copy in self.started:
            copy.wait_send()


FACTOR = HEAD ** (-0.5)
EXPONENT = FACTOR * 1.4426950408889634
F32 = jnp.float32
BF16 = jnp.bfloat16


def product(left, right):
    return jnp.dot(left, right, preferred_element_type=F32)


def product_rows(left, right):
    return lax.dot_general(left, right, (((1,), (1,)), ((), ())), preferred_element_type=F32)


def turn(field, cosine, sine):
    parts = []
    for head in range(2):
        one = field[:, head * HEAD : (head + 1) * HEAD]
        parts.append(one * cosine + pltpu.roll(one, HEAD // 2, 1) * sine)
    return jnp.concatenate(parts, axis=1)


def softmax_down(keys, queries):
    scores = product_rows(keys, queries)
    ahead = lax.broadcasted_iota(jnp.int32, (256, 256), 0) > lax.broadcasted_iota(jnp.int32, (256, 256), 1)
    own = jnp.where(ahead, -jnp.inf, scores[-256:])
    scores = own if scores.shape[0] == 256 else jnp.concatenate([scores[:-256], own], axis=0)
    highest = jnp.max(scores, axis=0, keepdims=True)
    raised = jnp.exp2((scores - highest) * EXPONENT)
    return raised * (1.0 / jnp.sum(raised, axis=0, keepdims=True))


def columns(head):
    return pl.ds(pl.multiple_of(head * HEAD, HEAD), HEAD)


def base_head(head, query, cotangent, keys, values, key_sum, value_sum):
    group = head // 8
    for block in range(2):
        rows, count = pl.ds(block * 256, 256), (block + 1) * 256
        queries, pulls = query[rows, columns(head)], cotangent[rows, columns(head)]
        weights = softmax_down(keys[:count, columns(group)], queries)
        pulled = product_rows(values[:count, columns(group)], pulls)
        mean = jnp.sum(weights * pulled, axis=0, keepdims=True)
        back = (weights * (pulled - mean) * FACTOR).astype(BF16)
        value_sum[:count, columns(group)] += product(weights.astype(BF16), pulls)
        key_sum[:count, columns(group)] += product(back, queries)


def tangent_head(head, query, tangent, keys, key_tangent, turned, context, context_tangent):
    group = head // 8
    for block in range(2):
        rows, count = pl.ds(block * 256, 256), (block + 1) * 256
        queries = query[rows, columns(head)]
        weights = softmax_down(keys[:count, columns(group)], queries)
        both_keys = jnp.concatenate([keys[:count, columns(group)], key_tangent[:count, columns(group)]], axis=1)
        both_queries = jnp.concatenate([tangent[rows, columns(head)], queries], axis=1)
        spread = product_rows(both_keys, both_queries)
        mean = jnp.sum(weights * spread, axis=0, keepdims=True)
        moved = (weights * (spread - mean) * FACTOR).astype(BF16)
        first = product(turned[group, :, :count], weights.astype(BF16))
        second = product(turned[group, :HEAD, :count], moved)
        context[rows, columns(head)] = first[:HEAD].T.astype(BF16)
        context_tangent[rows, columns(head)] = (first[HEAD:] + second).T.astype(BF16)


def project(normed, start, weights, total):
    total[...] = jnp.zeros_like(total)

    def step(at, carry):
        for kind, weight in enumerate(weights):
            sums = 0.0
            for part in range(4):
                index = at * 4 + part
                left = normed[pl.ds(start, 512), pl.ds(pl.multiple_of(index * 256, 256), 256)]
                sums = sums + product(left, weight[index])
            total[:, kind * 256 : (kind + 1) * 256] += sums
        return carry

    lax.fori_loop(0, 8, step, 0)


def layer_kernel(
    tokens, gain, query_in, tangent_in, kv_in, bias, task_in, bias_task, cotangent_in, cosine, sine,
    context, context_tangent, grad, bias_grad,
    token_rows, query, tangent, cotangent, normed, base_all, task_own, task_all, part, land, total, task_total,
    keys, values, kv_tangent, tangent_out, turned, key_sum, value_sum, back, back_kind, sums, sums_land,
    local, base_send, base_recv, task_send, task_recv, rows_send, rows_recv,
    part_send, part_recv, sums_send, sums_recv, pass_send, pass_recv,
):
    place = Place()
    h = place.h

    def load(source, target, at):
        copy = pltpu.make_async_copy(source, target, local.at[at])
        copy.start()
        return copy

    waits = [load(kv_in.at[kind], base_all.at[kind, place.dp], kind) for kind in range(2)]
    waits.append(load(task_in, task_own, 2))
    waits.append(load(task_in.at[h], task_all.at[place.dp], 3))
    waits.append(load(tokens, token_rows, 4))
    later = [load(query_in, query, 5), load(cotangent_in, cotangent, 6), load(tangent_in, tangent, 7)]
    greet(ring_devices(place) + [place.core_partner(), place.pair_chip(), place.other_chip()])
    for copy in waits:
        copy.wait()

    def base_piece(kind, index):
        return base_all.at[kind, index]

    def task_piece(kind, index):
        return task_all.at[index, pl.ds(kind * 128, 128), :]

    def task_partner(kind):
        return task_own.at[1 - h, pl.ds(kind * 128, 128), :]

    base = Gather(place, base_piece, lambda kind: base_piece(kind, place.dp), base_send, base_recv)
    task = Gather(place, task_piece, task_partner, task_send, task_recv)
    rows = Rows(place, normed, rows_send, rows_recv)
    base.first()

    scale = gain[...]
    for chunk in range(128 // CHUNK):

        def norm(at, carry, chunk=chunk):
            here = pl.multiple_of(chunk * CHUNK + at * 16, 16)
            wide = token_rows[pl.ds(here, 16), :].astype(F32)
            mean = jnp.mean(wide * wide, axis=-1, keepdims=True)
            there = pl.multiple_of(rows.mine * 128 + here, 16)
            normed[pl.ds(there, 16), :] = (wide * lax.rsqrt(mean + 1e-06) * scale).astype(BF16)
            return carry

        lax.fori_loop(0, CHUNK // 16, norm, 0)
        rows.own(chunk)
    for copy in later:
        copy.wait()

    chunks = list(range(128 // CHUNK))
    for at, (_, _, event) in enumerate(base.events()):
        event()
        if at in (9, 16, 23):
            rows.arrive(chunks.pop(0))
    task.first()
    for chunk in chunks:
        rows.arrive(chunk)
    for chunk in range(128 // CHUNK):
        rows.relay(chunk)
    rows.rest([rows.mine, rows.pair])
    ahead = [event for _, _, event in task.events()]

    def events(count):
        for _ in range(min(count, len(ahead))):
            ahead.pop(0)()

    mine, others = pl.multiple_of(h * 512, 512), pl.multiple_of(512 - h * 512, 512)
    project(normed, mine, [base_all.at[0], base_all.at[1]], total)
    events(6)
    keys[...] = turn(total[:, :256] + bias[0:1, :], cosine[...], sine[...]).astype(BF16)
    values[...] = (total[:, 256:] + bias[1:2, :]).astype(BF16)
    key_sum[...] = jnp.zeros_like(key_sum)
    value_sum[...] = jnp.zeros_like(value_sum)
    for quarter in range(4):

        def base_step(at, carry, quarter=quarter):
            base_head(quarter * 4 + at, query, cotangent, keys, values, key_sum, value_sum)
            return carry

        lax.fori_loop(0, 4, base_step, 0, unroll=4)
        events(6)

    key_back = turn(key_sum[...], cosine[...], -sine[...]).astype(BF16)
    value_back = value_sum[...].astype(BF16)
    back[0] = key_back.astype(F32).T.astype(BF16)
    back[1] = value_back.astype(F32).T.astype(BF16)

    def swap(source, target, at):
        return pltpu.make_async_remote_copy(
            src_ref=source,
            dst_ref=target,
            send_sem=pass_send.at[at],
            recv_sem=pass_recv.at[at],
            device_id=place.partner(),
            device_id_type=MESH,
        )

    back_swap = swap(back.at[1 - h], back_kind.at[h], 0)
    back_swap.start()
    back_kind[h] = back[h]
    sums[0] = jnp.zeros_like(sums[0])
    sums[0, 0:1, :] = jnp.sum(key_back.astype(F32), axis=0, keepdims=True)
    sums[0, 1:2, :] = jnp.sum(value_back.astype(F32), axis=0, keepdims=True)

    odd_y, odd_z = place.y % 2, place.z % 2
    mates = [
        place.device(0, 1 - 2 * odd_y, 0),
        place.device(0, 2 * odd_y - 1, 0),
        place.device(1, 1 - 2 * odd_z, 0),
        place.device(1, 2 * odd_z - 1, 0),
        place.partner(),
    ]

    def mate_copy(at):
        return pltpu.make_async_remote_copy(
            src_ref=sums.at[at],
            dst_ref=sums_land.at[at],
            send_sem=sums_send.at[at],
            recv_sem=sums_recv.at[at],
            device_id=mates[at],
            device_id_type=MESH,
        )

    def mate_sum(at):
        mate_copy(at).wait()
        sums[at + 1] = sums[at] + sums_land[at]
        if at + 1 < 5:
            mate_copy(at + 1).start()

    mate_copy(0).start()
    events(len(ahead))

    is_key = (h == 0).astype(F32)
    kind_cosine = cosine[...] * is_key + (1.0 - is_key)
    kind_sine = sine[...] * is_key
    kind_bias = jnp.where(h == 0, bias_task[0:1, :], bias_task[1:2, :])
    project(normed, mine, [task_all], task_total)
    kv_tangent[h] = turn(task_total[...] + kind_bias, kind_cosine, kind_sine).astype(BF16)
    for chunk in range(128 // CHUNK):
        rows.arrive_far(chunk)
    rows.rest([rows.other, rows.far])
    project(normed, others, [task_all], task_total)
    tangent_out[...] = turn(task_total[...] + kind_bias, kind_cosine, kind_sine).astype(BF16)
    tangent_swap = swap(tangent_out, kv_tangent.at[h], 1)
    tangent_swap.start()
    back_swap.wait_recv()

    scatter = Scatter(place, part, land, part_send, part_recv)

    def gradients(count, offsets):
        def step(at, carry):
            off_y, off_z = offsets(at)
            index = ((place.z + off_z) % 4) * 8 + ((place.y + off_y) % 4) * 2
            pick = pl.ds(pl.multiple_of(index * 256, 512), 512)
            block = product(back_kind[0], normed[:512, pick]) + product(back_kind[1], normed[512:, pick])
            block = block.astype(BF16)
            part[index] = block[:, :256]
            part[index + 1] = block[:, 256:]
            return carry

        lax.fori_loop(0, count, step, 0)

    gradients(4, lambda at: (2, at))
    scatter.first(0)
    gradients(3, lambda at: (3 + at, 2))
    scatter.first(1)
    gradients(6, lambda at: (1 + 2 * (at // 3), 3 + at % 3))
    scatter.second_own(0)
    gradients(3, lambda at: (0, 3 + at))
    scatter.second_own(1)

    def tangents(start, count):
        def step(at, carry):
            tangent_head(start + at, query, tangent, keys, kv_tangent.at[0], turned, context, context_tangent)
            return carry

        lax.fori_loop(0, count, step, 0, unroll=count)

    mate_sum(0)
    for across in (2, 1, 3, 0):
        for kind in range(2):
            scatter.second(kind, across)
    mate_sum(1)
    tangent_swap.wait_recv()
    for group in range(2):
        pick = slice(group * HEAD, (group + 1) * HEAD)
        turned[group, :HEAD, :] = values[:, pick].astype(F32).T.astype(BF16)
        turned[group, HEAD:, :] = kv_tangent[1, :, pick].astype(F32).T.astype(BF16)
    tangents(0, 4)
    mate_sum(2)
    for across in (2, 1, 3, 0):
        for kind in range(2):
            scatter.third(kind, across)
    tangents(4, 4)
    mate_sum(3)
    for kind in range(2):
        scatter.fourth(kind)
    tangents(8, 4)
    mate_sum(4)
    for kind in range(2):
        scatter.fifth(kind, grad)
    tangents(12, 4)
    for kind in range(2):
        scatter.last(kind, grad)
    bias_grad[...] = sums[5, 0:2, :]
    scatter.finish()
    base.finish()
    task.finish()
    rows.finish()
    back_swap.wait_send()
    tangent_swap.wait_send()


def layer(*operands):
    vmem = pl.BlockSpec(memory_space=pltpu.VMEM)
    hbm = pl.BlockSpec(memory_space=pl.ANY)
    scratch = [
        pltpu.VMEM((128, 8192), BF16),
        pltpu.VMEM((512, 2048), BF16),
        pltpu.VMEM((512, 2048), BF16),
        pltpu.VMEM((512, 2048), BF16),
        pltpu.VMEM((1024, 8192), BF16),
        pltpu.VMEM((2, 32, 256, 256), BF16),
        pltpu.VMEM((2, 256, 256), BF16),
        pltpu.VMEM((32, 256, 256), BF16),
        pltpu.VMEM((32, 256, 256), BF16),
        pltpu.VMEM((2, 31, 128, 256), BF16),
        pltpu.VMEM((512, 512), F32),
        pltpu.VMEM((512, 256), F32),
        pltpu.VMEM((512, 256), BF16),
        pltpu.VMEM((512, 256), BF16),
        pltpu.VMEM((2, 512, 256), BF16),
        pltpu.VMEM((512, 256), BF16),
        pltpu.VMEM((2, 256, 512), BF16),
        pltpu.VMEM((512, 256), F32),
        pltpu.VMEM((512, 256), F32),
        pltpu.VMEM((2, 256, 512), BF16),
        pltpu.VMEM((2, 256, 512), BF16),
        pltpu.VMEM((6, 8, 256), F32),
        pltpu.VMEM((5, 8, 256), F32),
        pltpu.SemaphoreType.DMA((8,)),
        *GATHER_SEMS,
        *GATHER_SEMS,
        *ROWS_SEMS,
        pltpu.SemaphoreType.DMA((2, 31)),
        pltpu.SemaphoreType.DMA((2, 31)),
        pltpu.SemaphoreType.DMA((5,)),
        pltpu.SemaphoreType.DMA((5,)),
        pltpu.SemaphoreType.DMA((2,)),
        pltpu.SemaphoreType.DMA((2,)),
    ]
    return pl.pallas_call(
        layer_kernel,
        out_shape=(
            jax.ShapeDtypeStruct((512, 2048), BF16),
            jax.ShapeDtypeStruct((512, 2048), BF16),
            jax.ShapeDtypeStruct((2, 256, 256), F32),
            jax.ShapeDtypeStruct((2, 256), F32),
        ),
        in_specs=[hbm, vmem, hbm, hbm, hbm, vmem, hbm, vmem, hbm, vmem, vmem],
        out_specs=(vmem,) * 4,
        scratch_shapes=scratch,
        compiler_params=pltpu.CompilerParams(
            collective_id=0, has_side_effects=True, vmem_limit_bytes=62 * 1024 * 1024
        ),
        name="layer",
    )(*operands)


def turning_tables():
    position = np.arange(512, dtype=np.float64)[:, None]
    frequency = 1000000.0 ** (-2.0 * np.arange(64) / 128)
    angle = position * frequency[None, :]
    cosine, sine = np.cos(angle), np.sin(angle)
    return (
        np.concatenate([cosine, cosine], axis=1).astype(np.float32),
        np.concatenate([-sine, sine], axis=1).astype(np.float32),
    )


def body(tokens, gain, query, query_tangent, kv_weight, kv_bias, kv_task, kv_bias_task, cotangent):
    cosine, sine = turning_tables()
    return layer(
        tokens, gain.reshape(1, -1), query, query_tangent, kv_weight, kv_bias, kv_task, kv_bias_task, cotangent,
        jnp.asarray(cosine), jnp.asarray(sine),
    )


def solution(mesh):
    in_specs = (
        P(("dp", "mp"), None),
        P(),
        P("dp", "mp"),
        P("dp", "mp"),
        P(None, "dp", "mp"),
        P(None, "mp"),
        P(None, "dp", "mp"),
        P(None, "mp"),
        P("dp", "mp"),
    )
    out_specs = (P("dp", "mp"), P("dp", "mp"), P(None, "dp", "mp"), P(None, "mp"))
    return jax.shard_map(body, mesh=mesh, in_specs=in_specs, out_specs=out_specs, check_vma=False)
```

```python
import functools

import jax
import jax.numpy as jnp
import numpy as np
from jax import lax
from jax.experimental import pallas as pl
from jax.experimental.pallas import tpu as pltpu
from jax.sharding import PartitionSpec as P

HEAD = 128
MESH = pl.DeviceIdType.MESH


class Place:
    def __init__(self):
        dp = lax.axis_index("dp")
        self.mp = lax.axis_index("mp")
        self.z, self.y, self.h = dp // 8, (dp // 2) % 4, dp % 2
        self.dp = dp

    def index(self, kind, along, across, half):
        dy, dz = (along, across) if kind == 0 else (across, along)
        return ((self.z + dz + 4) % 4) * 8 + ((self.y + dy + 4) % 4) * 2 + half

    def device(self, kind, along, across):
        return (self.index(kind, along, across, self.h), self.mp)

    def partner(self):
        return (self.dp + 1 - 2 * self.h, self.mp)

    def core_partner(self):
        return (self.dp, self.mp + 1 - 2 * (self.mp % 2))

    def pair_chip(self):
        return (self.dp, (self.mp + 2) % 4)

    def other_block(self):
        x = (self.h * 2 + self.mp // 2 + 2 * (self.mp // 2) + 3) % 4
        return x * 2 + self.mp % 2

    def other_chip(self):
        block = self.other_block()
        return (self.dp - self.h + block // 4, block % 4)


def greet(devices):
    barrier = pltpu.get_barrier_semaphore()
    for device in devices:
        pl.semaphore_signal(barrier, inc=1, device_id=device, device_id_type=MESH)


def greeted(devices):
    pl.semaphore_wait(pltpu.get_barrier_semaphore(), len(devices))


def ring_devices(place):
    return [
        place.device(0, 1, 0),
        place.device(0, -1, 0),
        place.device(0, 0, 1),
        place.device(0, 0, -1),
        place.partner(),
    ]


def sent(amount, semaphore, place):
    pltpu.make_async_remote_copy(
        src_ref=amount,
        dst_ref=amount,
        send_sem=semaphore,
        recv_sem=semaphore,
        device_id=place.partner(),
        device_id_type=MESH,
    ).wait_send()


class Gather:
    def __init__(self, place, piece, partner_piece, sent, send, recv):
        self.place, self.piece, self.partner_piece, self.sent = place, piece, partner_piece, sent
        self.send, self.recv = send, recv

    def copy(self, kind, index, device, source=None):
        block = self.piece(kind, index)
        return pltpu.make_async_remote_copy(
            src_ref=block if source is None else source,
            dst_ref=block,
            send_sem=self.send.at[kind],
            recv_sem=self.recv.at[kind, index // 2],
            device_id=device,
            device_id_type=MESH,
        )

    def start(self, kind, index, device, source=None):
        self.copy(kind, index, device, source).start()

    def wait(self, kind, along, across):
        index = self.place.index(kind, along, across, 0)
        amount = self.sent(kind, 2)
        pltpu.make_async_remote_copy(
            src_ref=amount,
            dst_ref=amount,
            send_sem=self.send.at[kind],
            recv_sem=self.recv.at[kind, index // 2],
            device_id=self.place.partner(),
            device_id_type=MESH,
        ).wait_recv()

    def spread(self, kind, index, along):
        if along:
            self.start(kind, index, self.place.device(kind, 1, 0))
            self.start(kind, index, self.place.device(kind, -1, 0))
        self.start(kind, index, self.place.device(kind, 0, 1))
        self.start(kind, index, self.place.device(kind, 0, -1))

    def swap(self):
        for kind in range(2):
            self.start(kind, self.place.dp, self.place.partner(), self.partner_piece(kind))

    def first(self):
        own = self.place.dp
        for kind in range(2):
            self.spread(kind, own, True)

    def events(self):
        place = self.place

        def partner(kind):
            other = place.index(kind, 0, 0, 1 - place.h)
            self.copy(kind, other, place.partner()).wait_recv()
            self.spread(kind, other, True)

        def side_relay(kind, along):
            self.wait(kind, along, 0)
            near = 0 if along < 0 else 1
            self.start(kind, place.index(kind, along, 0, near), place.device(kind, -along, 0))

        def side_spread(kind, along):
            for half in range(2):
                self.spread(kind, place.index(kind, along, 0, half), False)

        def opposite(kind):
            self.wait(kind, 2, 0)
            for half in range(2):
                self.spread(kind, place.index(kind, 2, 0, half), False)

        def across(kind, along, step):
            self.wait(kind, along, step)
            near = 0 if step < 0 else 1
            self.start(kind, place.index(kind, along, step, near), place.device(kind, 0, -step))

        def across_opposite(kind, along):
            self.wait(kind, along, 2)

        result = []

        def add(blocks, function, *rest):
            for kind in range(2):
                result.append((kind, blocks, functools.partial(function, kind, *rest)))

        add([(0, 0)], partner)
        add([(-1, 0)], side_relay, -1)
        add([(1, 0)], side_relay, 1)
        add([], side_spread, -1)
        add([], side_spread, 1)
        add([(0, -1)], across, 0, -1)
        add([(0, 1)], across, 0, 1)
        add([(2, 0)], opposite)
        for along in (-1, 1, 2):
            add([(along, -1)], across, along, -1)
            add([(along, 1)], across, along, 1)
            before = {-1: 0, 1: -1, 2: 1}[along]
            add([(before, 2)], across_opposite, before)
        add([(2, 2)], across_opposite, 2)
        return result

    def finish(self):
        for kind in range(2):
            sent(self.sent(kind, 31), self.send.at[kind], self.place)


GATHER_SEMS = [pltpu.SemaphoreType.DMA((2,)), pltpu.SemaphoreType.DMA((2, 16))]
CHUNKS = 8
CHUNK = 8192 // CHUNKS


class Rows:
    def __init__(self, place, whole, send, recv):
        self.place, self.whole, self.send, self.recv = place, whole, send, recv
        mp, h = place.mp, place.h
        self.mine = h * 4 + mp
        self.pair = h * 4 + (mp + 2) % 4
        self.other = place.other_block()
        x = (h * 2 + mp // 2 + 2) % 4
        self.far = x * 2 + mp % 2

    def copy(self, owner, chunk, device, lane):
        rows = pl.ds(pl.multiple_of(owner * 128, 128), 128)
        block = self.whole.at[rows, pl.ds(chunk * CHUNK, CHUNK)]
        return pltpu.make_async_remote_copy(
            src_ref=block,
            dst_ref=block,
            send_sem=self.send.at[lane],
            recv_sem=self.recv.at[owner, chunk],
            device_id=device,
            device_id_type=MESH,
        )

    def start(self, owner, chunk, device, lane):
        self.copy(owner, chunk, device, lane).start()

    def own(self, chunk):
        self.start(self.mine, chunk, self.place.pair_chip(), 0)
        self.start(self.mine, chunk, self.place.other_chip(), 1)
        self.start(self.mine, chunk, self.place.core_partner(), 2)

    def wait(self, owner, chunk):
        self.copy(owner, chunk, self.place.core_partner(), 0).wait_recv()

    def arrive_pair(self, chunk):
        self.wait(self.pair, chunk)
        self.start(self.pair, chunk, self.place.core_partner(), 3)

    def arrive_other(self, chunk):
        self.wait(self.other, chunk)
        self.start(self.other, chunk, self.place.core_partner(), 4)

    def relay(self, chunk):
        if chunk < CHUNKS // 2:
            self.start(self.pair, chunk, self.place.other_chip(), 5)
        else:
            self.start(self.other, chunk, self.place.pair_chip(), 5)

    def arrive_far(self, chunk):
        self.wait(self.far, chunk)
        self.start(self.far, chunk, self.place.core_partner(), 6)

    def rest(self, owners, chunk):
        for owner in owners:
            self.wait(owner + 1 - 2 * (owner % 2), chunk)

    def finish(self):
        for lane in range(7):
            sent(self.whole.at[pl.ds(0, 128), :], self.send.at[lane], self.place)


ROWS_SEMS = [pltpu.SemaphoreType.DMA((7,)), pltpu.SemaphoreType.DMA((8, CHUNKS))]


class Scatter:
    def __init__(self, place, part, land, send, recv):
        self.place, self.part, self.land, self.send, self.recv = place, part, land, send, recv

    def own(self, kind, along, across, half):
        return self.part.at[self.place.index(kind, along, across, half), pl.ds(kind * 128, 128), :]

    def copy(self, kind, block, spot, device):
        return pltpu.make_async_remote_copy(
            src_ref=block,
            dst_ref=self.land.at[kind, spot],
            send_sem=self.send.at[kind],
            recv_sem=self.recv.at[kind, self.lane(spot)],
            device_id=device,
            device_id_type=MESH,
        )

    @staticmethod
    def lane(spot):
        if 16 <= spot < 24:
            return spot - 8
        return spot - 2 if spot in (28, 29) else spot

    def start(self, kind, block, spot, device):
        self.copy(kind, block, spot, device).start()

    def wait(self, kind, spots):
        amount = self.land.at[kind, pl.ds(0, len(spots))]
        pltpu.make_async_remote_copy(
            src_ref=amount,
            dst_ref=amount,
            send_sem=self.send.at[kind],
            recv_sem=self.recv.at[kind, self.lane(spots[0])],
            device_id=self.place.partner(),
            device_id_type=MESH,
        ).wait_recv()

    def add(self, kind, block, spots):
        self.wait(kind, spots)

        def step(at, carry):
            rows = pl.ds(pl.multiple_of(at * 64, 64), 64)
            total = block[rows, :].astype(jnp.float32)
            for spot in spots:
                total = total + self.land[kind, spot, rows, :].astype(jnp.float32)
            block[rows, :] = total.astype(jnp.bfloat16)
            return carry

        lax.fori_loop(0, 2, step, 0)

    def first(self, kind):
        for across in (2, 1, 3, 0):
            for half, along in ((0, 1), (1, -1)):
                block = self.own(kind, 2, across, half)
                self.start(kind, block, half * 4 + across, self.place.device(kind, along, 0))

    def second_own(self, kind, across):
        for side, along in ((0, 1), (1, -1)):
            half = 1 - side
            block = self.own(kind, along, across, half)
            spot = 8 + side * 8 + across * 2 + half
            self.start(kind, block, spot, self.place.device(kind, along, 0))

    def second(self, kind, across):
        for side, along in ((0, 1), (1, -1)):
            half = side
            block = self.own(kind, along, across, half)
            self.add(kind, block, [side * 4 + across])
            spot = 8 + side * 8 + across * 2 + half
            self.start(kind, block, spot, self.place.device(kind, along, 0))

    def third(self, kind, across):
        for half in range(2):
            block = self.own(kind, 0, across, half)
            self.add(kind, block, [8 + across * 2 + half, 16 + across * 2 + half])
            if across == 2:
                along = 1 if half == 0 else -1
                self.start(kind, block, 24 + half, self.place.device(kind, 0, along))
            if across in (1, 3):
                side = 0 if across == 1 else 1
                if half != side:
                    along = 1 if side == 0 else -1
                    self.start(kind, block, 26 + side * 2 + half, self.place.device(kind, 0, along))

    def fourth(self, kind):
        for side, across in ((0, 1), (1, 3)):
            block = self.own(kind, 0, across, side)
            self.add(kind, block, [24 + side])
            along = 1 if side == 0 else -1
            self.start(kind, block, 26 + side * 2 + side, self.place.device(kind, 0, along))

    def fifth(self, kind, grad):
        for half in (1 - self.place.h, self.place.h):
            self.wait_last(kind, half)
        block = self.own(kind, 0, 0, 1 - self.place.h)
        block[...] = self.summed(kind, 1 - self.place.h).astype(jnp.bfloat16)
        self.start(kind, block, 30, self.place.partner())
        grad[self.place.h, :, kind * 128 : (kind + 1) * 128] = self.summed(kind, self.place.h).T

    def wait_last(self, kind, half):
        amount = self.land.at[kind, pl.ds(0, 2)]
        pltpu.make_async_remote_copy(
            src_ref=amount,
            dst_ref=amount,
            send_sem=self.send.at[kind],
            recv_sem=self.recv.at[kind, 26 + half],
            device_id=self.place.partner(),
            device_id_type=MESH,
        ).wait_recv()

    def summed(self, kind, half):
        total = self.own(kind, 0, 0, half)[...].astype(jnp.float32)
        for side in range(2):
            total = total + self.land[kind, 26 + side * 2 + half].astype(jnp.float32)
        return total

    def last(self, kind, grad):
        self.wait(kind, [30])
        block = self.land[kind, 30].astype(jnp.float32)
        grad[1 - self.place.h, :, kind * 128 : (kind + 1) * 128] = block.T

    def finish(self):
        for kind in range(2):
            sent(self.land.at[kind], self.send.at[kind], self.place)


FACTOR = HEAD ** (-0.5)
EXPONENT = FACTOR * 1.4426950408889634
F32 = jnp.float32
BF16 = jnp.bfloat16


def product(left, right):
    return jnp.dot(left, right, preferred_element_type=F32)


def product_rows(left, right):
    return lax.dot_general(left, right, (((1,), (1,)), ((), ())), preferred_element_type=F32)


def turn(field, cosine, sine):
    parts = []
    for head in range(2):
        one = field[:, head * HEAD : (head + 1) * HEAD]
        parts.append(one * cosine + pltpu.roll(one, HEAD // 2, 1) * sine)
    return jnp.concatenate(parts, axis=1)


def softmax_down(keys, queries):
    scores = product_rows(keys, queries)
    ahead = lax.broadcasted_iota(jnp.int32, (256, 256), 0) > lax.broadcasted_iota(jnp.int32, (256, 256), 1)
    own = jnp.where(ahead, -jnp.inf, scores[-256:])
    scores = own if scores.shape[0] == 256 else jnp.concatenate([scores[:-256], own], axis=0)
    highest = jnp.max(scores, axis=0, keepdims=True)
    raised = jnp.exp2((scores - highest) * EXPONENT)
    return raised * (1.0 / jnp.sum(raised, axis=0, keepdims=True))


def columns(head):
    return pl.ds(pl.multiple_of(head * HEAD, HEAD), HEAD)


def base_head(head, query, cotangent, keys, values, key_sum, value_sum):
    group = head // 8
    for block in range(2):
        rows, count = pl.ds(block * 256, 256), (block + 1) * 256
        queries, pulls = query[rows, columns(head)], cotangent[rows, columns(head)]
        weights = softmax_down(keys[:count, columns(group)], queries)
        pulled = product_rows(values[:count, columns(group)], pulls)
        mean = jnp.sum(weights * pulled, axis=0, keepdims=True)
        back = (weights * (pulled - mean) * FACTOR).astype(BF16)
        value_sum[:count, columns(group)] += product(weights.astype(BF16), pulls)
        key_sum[:count, columns(group)] += product(back, queries)


def tangent_head(head, query, tangent, keys, key_tangent, turned, context, context_tangent):
    group = head // 8
    for block in range(2):
        rows, count = pl.ds(block * 256, 256), (block + 1) * 256
        queries = query[rows, columns(head)]
        weights = softmax_down(keys[:count, columns(group)], queries)
        both_keys = jnp.concatenate([keys[:count, columns(group)], key_tangent[:count, columns(group)]], axis=1)
        both_queries = jnp.concatenate([tangent[rows, columns(head)], queries], axis=1)
        spread = product_rows(both_keys, both_queries)
        mean = jnp.sum(weights * spread, axis=0, keepdims=True)
        moved = (weights * (spread - mean) * FACTOR).astype(BF16)
        first = product(turned[group, :, :count], weights.astype(BF16))
        second = product(turned[group, :HEAD, :count], moved)
        context[rows, columns(head)] = first[:HEAD].T.astype(BF16)
        context_tangent[rows, columns(head)] = (first[HEAD:] + second).T.astype(BF16)


def project(normed, start, weights, total, first, last):
    def step(at, carry):
        for kind, weight in enumerate(weights):
            sums = 0.0
            for part in range(4):
                index = at * 4 + part
                left = normed[pl.ds(start, 512), pl.ds(pl.multiple_of(index * 256, 256), 256)]
                sums = sums + product(left, weight[index])
            total[:, kind * 256 : (kind + 1) * 256] += sums
        return carry

    lax.fori_loop(first, last, step, 0)


def layer_kernel(
    tokens, gain, query_in, tangent_in, kv_in, bias, task_in, bias_task, cotangent_in, cosine, sine,
    context_out, context_tangent_out, grad, bias_grad,
    context, context_tangent, token_rows, query, tangent, cotangent, normed, base_all, task_own, task_all, part, land, total, task_total,
    keys, values, kv_tangent, tangent_out, turned, key_sum, value_sum, back, back_kind, sums, sums_land,
    local, out_sems, base_send, base_recv, task_send, task_recv, rows_send, rows_recv,
    part_send, part_recv, sums_send, sums_recv, pass_send, pass_recv,
):
    place = Place()
    h = place.h

    def load(source, target, at):
        copy = pltpu.make_async_copy(source, target, local.at[at])
        copy.start()
        return copy

    waits = [load(kv_in.at[kind], base_all.at[kind, place.dp], kind) for kind in range(2)]
    waits.append(load(task_in, task_own, 2))
    waits.append(load(task_in.at[h], task_all.at[place.dp], 3))
    load_tokens = load(tokens, token_rows, 4)
    later = [load(query_in, query, 5), load(cotangent_in, cotangent, 6), load(tangent_in, tangent, 7)]
    around = ring_devices(place) + [place.core_partner(), place.pair_chip(), place.other_chip()]
    greet(around)

    def base_piece(kind, index):
        return base_all.at[kind, index]

    def task_piece(kind, index):
        return task_all.at[index, pl.ds(kind * 128, 128), :]

    def task_partner(kind):
        return task_own.at[1 - h, pl.ds(kind * 128, 128), :]

    base = Gather(
        place, base_piece, lambda kind: base_piece(kind, place.dp),
        lambda kind, count: base_all.at[kind, pl.ds(0, count)], base_send, base_recv,
    )
    task = Gather(
        place, task_piece, task_partner,
        lambda kind, count: task_all.at[pl.ds(0, count), pl.ds(0, 128), :], task_send, task_recv,
    )
    rows = Rows(place, normed, rows_send, rows_recv)
    for copy in waits:
        copy.wait()
    greeted(around)
    base.swap()
    task.swap()
    base.first()
    load_tokens.wait()
    scale = gain[...]

    def norm(at, carry):
        here = pl.multiple_of(at * 16, 16)
        wide = token_rows[pl.ds(here, 16), :].astype(F32)
        mean = jnp.mean(wide * wide, axis=-1, keepdims=True)
        there = pl.multiple_of(rows.mine * 128 + here, 16)
        normed[pl.ds(there, 16), :] = (wide * lax.rsqrt(mean + 1e-06) * scale).astype(BF16)
        return carry

    lax.fori_loop(0, 8, norm, 0)
    for chunk in range(CHUNKS):
        rows.own(chunk)
    for copy in later:
        copy.wait()

    for at, (_, _, event) in enumerate(base.events()):
        event()
        if at in (16, 19, 22, 26, 31):
            chunk = (16, 19, 22, 26, 31).index(at)
            rows.arrive_pair(chunk)
            if chunk > 0:
                rows.arrive_other(chunk - 1)
    task.first()
    ahead = [event for _, _, event in task.events()]

    def events(count):
        for _ in range(min(count, len(ahead))):
            ahead.pop(0)()

    events(2)
    mine, others = pl.multiple_of(h * 512, 512), pl.multiple_of(512 - h * 512, 512)
    total[...] = jnp.zeros_like(total)
    both = [base_all.at[0], base_all.at[1]]
    rows.arrive_pair(5)
    for chunk in range(4):
        rows.rest([rows.mine, rows.pair], chunk)
    project(normed, mine, both, total, 0, 4)
    for chunk in (4, 5, 6, 7):
        if chunk >= 6:
            rows.arrive_pair(chunk)
        if chunk == 7:
            for other in range(CHUNKS // 2):
                rows.relay(other)
            for other in range(4, 7):
                rows.arrive_other(other)
                rows.relay(other)
        rows.rest([rows.mine, rows.pair], chunk)
        project(normed, mine, both, total, chunk, chunk + 1)
    rows.arrive_other(7)
    rows.relay(7)
    keys[...] = turn(total[:, :256] + bias[0:1, :], cosine[...], sine[...]).astype(BF16)
    values[...] = (total[:, 256:] + bias[1:2, :]).astype(BF16)
    events(8)
    key_sum[...] = jnp.zeros_like(key_sum)
    value_sum[...] = jnp.zeros_like(value_sum)
    for part_of in range(8):

        def base_step(at, carry, part_of=part_of):
            base_head(part_of * 2 + at, query, cotangent, keys, values, key_sum, value_sum)
            return carry

        lax.fori_loop(0, 2, base_step, 0, unroll=2)
        events((4, 0, 2, 4, 2, 4, 4, 4)[part_of])
        for chunk in ((), (), (), (), (), (0, 4), (), (1, 5))[part_of]:
            rows.arrive_far(chunk)

    key_back = turn(key_sum[...], cosine[...], -sine[...]).astype(BF16)
    value_back = value_sum[...].astype(BF16)
    back[0] = key_back.astype(F32).T.astype(BF16)
    back[1] = value_back.astype(F32).T.astype(BF16)

    def swap(source, target, at):
        return pltpu.make_async_remote_copy(
            src_ref=source,
            dst_ref=target,
            send_sem=pass_send.at[at],
            recv_sem=pass_recv.at[at],
            device_id=place.partner(),
            device_id_type=MESH,
        )

    back_swap = swap(back.at[1 - h], back_kind.at[h], 0)
    back_swap.start()
    back_kind[h] = back[h]
    sums[0] = jnp.zeros_like(sums[0])
    sums[0, 0:1, :] = jnp.sum(key_back.astype(F32), axis=0, keepdims=True)
    sums[0, 1:2, :] = jnp.sum(value_back.astype(F32), axis=0, keepdims=True)

    odd_y, odd_z = place.y % 2, place.z % 2
    mates = [
        place.device(0, 1 - 2 * odd_y, 0),
        place.device(0, 2 * odd_y - 1, 0),
        place.device(1, 1 - 2 * odd_z, 0),
        place.device(1, 2 * odd_z - 1, 0),
        place.partner(),
    ]

    def mate_copy(at):
        return pltpu.make_async_remote_copy(
            src_ref=sums.at[at],
            dst_ref=sums_land.at[at],
            send_sem=sums_send.at[at],
            recv_sem=sums_recv.at[at],
            device_id=mates[at],
            device_id_type=MESH,
        )

    def mate_sum(at):
        mate_copy(at).wait()
        sums[at + 1] = sums[at] + sums_land[at]
        if at + 1 < 5:
            mate_copy(at + 1).start()

    mate_copy(0).start()
    events(len(ahead))

    is_key = (h == 0).astype(F32)
    kind_cosine = cosine[...] * is_key + (1.0 - is_key)
    kind_sine = sine[...] * is_key
    kind_bias = jnp.where(h == 0, bias_task[0:1, :], bias_task[1:2, :])
    task_total[...] = jnp.zeros_like(task_total)
    project(normed, mine, [task_all], task_total, 0, 8)
    kv_tangent[h] = turn(task_total[...] + kind_bias, kind_cosine, kind_sine).astype(BF16)
    task_total[...] = jnp.zeros_like(task_total)

    def project_others(chunks):
        for chunk in chunks:
            rows.rest([rows.other, rows.far], chunk)
            project(normed, others, [task_all], task_total, chunk, chunk + 1)

    mate_sum(0)
    for chunk in (2, 6):
        rows.arrive_far(chunk)
    project_others((0, 1, 4, 5))
    mate_sum(1)
    for chunk in (3, 7):
        rows.arrive_far(chunk)
    project_others((2, 6))
    mate_sum(2)
    for chunk in (3, 7):
        rows.rest([rows.other, rows.far], chunk)
    back_swap.wait_recv()

    scatter = Scatter(place, part, land, part_send, part_recv)

    def gradients(count, offsets):
        def step(at, carry):
            off_y, off_z = offsets(at)
            index = ((place.z + off_z) % 4) * 8 + ((place.y + off_y) % 4) * 2
            pick = pl.ds(pl.multiple_of(index * 256, 512), 512)
            block = product(back_kind[0], normed[:512, pick]) + product(back_kind[1], normed[512:, pick])
            block = block.astype(BF16)
            part[index] = block[:, :256]
            part[index + 1] = block[:, 256:]
            return carry

        lax.fori_loop(0, count, step, 0)

    gradients(4, lambda at: (2, at))
    scatter.first(0)
    gradients(3, lambda at: (3 + at, 2))
    scatter.first(1)
    mate_sum(3)
    for chunk in (3, 7):
        project(normed, others, [task_all], task_total, chunk, chunk + 1)
    tangent_out[...] = turn(task_total[...] + kind_bias, kind_cosine, kind_sine).astype(BF16)
    tangent_swap = swap(tangent_out, kv_tangent.at[h], 1)
    tangent_swap.start()
    gradients(6, lambda at: (1 + 2 * (at // 3), 3 + at % 3))
    gradients(3, lambda at: (0, 3 + at))

    outs = []

    def tangents(start, count):
        def step(at, carry):
            tangent_head(start + at, query, tangent, keys, kv_tangent.at[0], turned, context, context_tangent)
            return carry

        lax.fori_loop(0, count, step, 0, unroll=count)
        pick = pl.ds(start * HEAD, count * HEAD)
        for source, target in ((context, context_out), (context_tangent, context_tangent_out)):
            outs.append(pltpu.make_async_copy(source.at[:, pick], target.at[:, pick], out_sems.at[len(outs)]))
            outs[-1].start()

    for across in (2, 1, 3, 0):
        for kind in range(2):
            scatter.second_own(kind, across)
        for kind in range(2):
            scatter.second(kind, across)
    tangent_swap.wait_recv()
    for group in range(2):
        pick = slice(group * HEAD, (group + 1) * HEAD)
        turned[group, :HEAD, :] = values[:, pick].astype(F32).T.astype(BF16)
        turned[group, HEAD:, :] = kv_tangent[1, :, pick].astype(F32).T.astype(BF16)
    def third(across):
        for kind in range(2):
            scatter.third(kind, across)

    tangents(0, 4)
    third(2)
    tangents(4, 4)
    third(1)
    third(3)
    tangents(8, 4)
    for kind in range(2):
        scatter.fourth(kind)
    third(0)
    for kind in range(2):
        scatter.fifth(kind, grad)
    tangents(12, 4)
    mate_sum(4)
    bias_grad[...] = sums[5, 0:2, :]
    for kind in range(2):
        scatter.last(kind, grad)
    for copy in outs:
        copy.wait()
    scatter.finish()
    base.finish()
    task.finish()
    rows.finish()
    back_swap.wait_send()
    tangent_swap.wait_send()


def layer(*operands):
    vmem = pl.BlockSpec(memory_space=pltpu.VMEM)
    hbm = pl.BlockSpec(memory_space=pl.ANY)
    scratch = [
        pltpu.VMEM((512, 2048), BF16),
        pltpu.VMEM((512, 2048), BF16),
        pltpu.VMEM((128, 8192), BF16),
        pltpu.VMEM((512, 2048), BF16),
        pltpu.VMEM((512, 2048), BF16),
        pltpu.VMEM((512, 2048), BF16),
        pltpu.VMEM((1024, 8192), BF16),
        pltpu.VMEM((2, 32, 256, 256), BF16),
        pltpu.VMEM((2, 256, 256), BF16),
        pltpu.VMEM((32, 256, 256), BF16),
        pltpu.VMEM((32, 256, 256), BF16),
        pltpu.VMEM((2, 31, 128, 256), BF16),
        pltpu.VMEM((512, 512), F32),
        pltpu.VMEM((512, 256), F32),
        pltpu.VMEM((512, 256), BF16),
        pltpu.VMEM((512, 256), BF16),
        pltpu.VMEM((2, 512, 256), BF16),
        pltpu.VMEM((512, 256), BF16),
        pltpu.VMEM((2, 256, 512), BF16),
        pltpu.VMEM((512, 256), F32),
        pltpu.VMEM((512, 256), F32),
        pltpu.VMEM((2, 256, 512), BF16),
        pltpu.VMEM((2, 256, 512), BF16),
        pltpu.VMEM((6, 8, 256), F32),
        pltpu.VMEM((5, 8, 256), F32),
        pltpu.SemaphoreType.DMA((8,)),
        pltpu.SemaphoreType.DMA((8,)),
        *GATHER_SEMS,
        *GATHER_SEMS,
        *ROWS_SEMS,
        pltpu.SemaphoreType.DMA((2,)),
        pltpu.SemaphoreType.DMA((2, 31)),
        pltpu.SemaphoreType.DMA((5,)),
        pltpu.SemaphoreType.DMA((5,)),
        pltpu.SemaphoreType.DMA((2,)),
        pltpu.SemaphoreType.DMA((2,)),
    ]
    return pl.pallas_call(
        layer_kernel,
        out_shape=(
            jax.ShapeDtypeStruct((512, 2048), BF16),
            jax.ShapeDtypeStruct((512, 2048), BF16),
            jax.ShapeDtypeStruct((2, 256, 256), F32),
            jax.ShapeDtypeStruct((2, 256), F32),
        ),
        in_specs=[hbm, vmem, hbm, hbm, hbm, vmem, hbm, vmem, hbm, vmem, vmem],
        out_specs=(hbm, hbm, vmem, vmem),
        scratch_shapes=scratch,
        compiler_params=pltpu.CompilerParams(
            collective_id=0, has_side_effects=True, vmem_limit_bytes=62 * 1024 * 1024
        ),
        name="layer",
    )(*operands)


def hand_over_kernel(context, context_tangent, grad, bias_grad, *rest):
    outs, held, loads, stores = rest[:4], rest[4:8], rest[8], rest[9]
    pieces = []
    for at in range(4):
        rows = pl.ds(at * 128, 128)
        for which, source in ((0, context), (1, context_tangent)):
            pieces.append((source.at[rows, :], held[which].at[rows, :], outs[which].at[rows, :]))
    pieces.append((grad, held[2], outs[2]))
    pieces.append((bias_grad, held[3], outs[3]))
    arriving = [pltpu.make_async_copy(a, b, loads.at[at]) for at, (a, b, _) in enumerate(pieces)]
    leaving = [pltpu.make_async_copy(b, c, stores.at[at]) for at, (_, b, c) in enumerate(pieces)]
    for copy in arriving:
        copy.start()
    for copy, after in zip(arriving, leaving):
        copy.wait()
        after.start()
    for copy in leaving:
        copy.wait()


def hand_over(*results):
    hbm = pl.BlockSpec(memory_space=pl.ANY)
    return pl.pallas_call(
        hand_over_kernel,
        out_shape=tuple(jax.ShapeDtypeStruct(one.shape, one.dtype) for one in results),
        in_specs=[hbm] * 4,
        out_specs=(hbm,) * 4,
        scratch_shapes=[pltpu.VMEM(one.shape, one.dtype) for one in results]
        + [pltpu.SemaphoreType.DMA((10,)), pltpu.SemaphoreType.DMA((10,))],
        compiler_params=pltpu.CompilerParams(vmem_limit_bytes=62 * 1024 * 1024),
        name="hand_over",
    )(*results)


def turning_tables():
    position = np.arange(512, dtype=np.float64)[:, None]
    frequency = 1000000.0 ** (-2.0 * np.arange(64) / 128)
    angle = position * frequency[None, :]
    cosine, sine = np.cos(angle), np.sin(angle)
    return (
        np.concatenate([cosine, cosine], axis=1).astype(np.float32),
        np.concatenate([-sine, sine], axis=1).astype(np.float32),
    )


def body(tokens, gain, query, query_tangent, kv_weight, kv_bias, kv_task, kv_bias_task, cotangent):
    cosine, sine = turning_tables()
    return hand_over(*layer(
        tokens, gain.reshape(1, -1), query, query_tangent, kv_weight, kv_bias, kv_task, kv_bias_task, cotangent,
        jnp.asarray(cosine), jnp.asarray(sine),
    ))


def solution(mesh):
    in_specs = (
        P(("dp", "mp"), None),
        P(),
        P("dp", "mp"),
        P("dp", "mp"),
        P(None, "dp", "mp"),
        P(None, "mp"),
        P(None, "dp", "mp"),
        P(None, "mp"),
        P("dp", "mp"),
    )
    out_specs = (P("dp", "mp"), P("dp", "mp"), P(None, "dp", "mp"), P(None, "mp"))
    return jax.shard_map(body, mesh=mesh, in_specs=in_specs, out_specs=out_specs, check_vma=False)
```

```python
import functools

import jax
import jax.numpy as jnp
import numpy as np
from jax import lax
from jax.experimental import pallas as pl
from jax.experimental.pallas import tpu as pltpu
from jax.sharding import PartitionSpec as P

HEAD = 128
MESH = pl.DeviceIdType.MESH


class Place:
    def __init__(self):
        dp = lax.axis_index("dp")
        self.mp = lax.axis_index("mp")
        self.z, self.y, self.h = dp // 8, (dp // 2) % 4, dp % 2
        self.dp = dp

    def index(self, kind, along, across, half):
        dy, dz = (along, across) if kind == 0 else (across, along)
        return ((self.z + dz + 4) % 4) * 8 + ((self.y + dy + 4) % 4) * 2 + half

    def device(self, kind, along, across):
        return (self.index(kind, along, across, self.h), self.mp)

    def partner(self):
        return (self.dp + 1 - 2 * self.h, self.mp)

    def core_partner(self):
        return (self.dp, self.mp + 1 - 2 * (self.mp % 2))

    def pair_chip(self):
        return (self.dp, (self.mp + 2) % 4)

    def other_block(self):
        x = (self.h * 2 + self.mp // 2 + 2 * (self.mp // 2) + 3) % 4
        return x * 2 + self.mp % 2

    def other_chip(self):
        block = self.other_block()
        return (self.dp - self.h + block // 4, block % 4)


def greet(devices):
    barrier = pltpu.get_barrier_semaphore()
    for device in devices:
        pl.semaphore_signal(barrier, inc=1, device_id=device, device_id_type=MESH)


def greeted(devices):
    pl.semaphore_wait(pltpu.get_barrier_semaphore(), len(devices))


def ring_devices(place):
    return [
        place.device(0, 1, 0),
        place.device(0, -1, 0),
        place.device(0, 0, 1),
        place.device(0, 0, -1),
        place.partner(),
    ]


def sent(amount, semaphore, place):
    pltpu.make_async_remote_copy(
        src_ref=amount,
        dst_ref=amount,
        send_sem=semaphore,
        recv_sem=semaphore,
        device_id=place.partner(),
        device_id_type=MESH,
    ).wait_send()


class Gather:
    def __init__(self, place, piece, partner_piece, sent, send, recv):
        self.place, self.piece, self.partner_piece, self.sent = place, piece, partner_piece, sent
        self.send, self.recv = send, recv

    def copy(self, kind, index, device, source=None):
        block = self.piece(kind, index)
        return pltpu.make_async_remote_copy(
            src_ref=block if source is None else source,
            dst_ref=block,
            send_sem=self.send.at[kind],
            recv_sem=self.recv.at[kind, index // 2],
            device_id=device,
            device_id_type=MESH,
        )

    def start(self, kind, index, device, source=None):
        self.copy(kind, index, device, source).start()

    def wait(self, kind, along, across):
        index = self.place.index(kind, along, across, 0)
        amount = self.sent(kind, 2)
        pltpu.make_async_remote_copy(
            src_ref=amount,
            dst_ref=amount,
            send_sem=self.send.at[kind],
            recv_sem=self.recv.at[kind, index // 2],
            device_id=self.place.partner(),
            device_id_type=MESH,
        ).wait_recv()

    def spread(self, kind, index, along):
        if along:
            self.start(kind, index, self.place.device(kind, 1, 0))
            self.start(kind, index, self.place.device(kind, -1, 0))
        self.start(kind, index, self.place.device(kind, 0, 1))
        self.start(kind, index, self.place.device(kind, 0, -1))

    def swap(self):
        for kind in range(2):
            self.start(kind, self.place.dp, self.place.partner(), self.partner_piece(kind))

    def first(self):
        own = self.place.dp
        for kind in range(2):
            self.spread(kind, own, True)

    def events(self):
        place = self.place

        def partner(kind):
            other = place.index(kind, 0, 0, 1 - place.h)
            if self.partner_piece is not None:
                self.copy(kind, other, place.partner()).wait_recv()
            self.spread(kind, other, True)

        def side_relay(kind, along):
            self.wait(kind, along, 0)
            near = 0 if along < 0 else 1
            self.start(kind, place.index(kind, along, 0, near), place.device(kind, -along, 0))

        def side_spread(kind, along):
            for half in range(2):
                self.spread(kind, place.index(kind, along, 0, half), False)

        def opposite(kind):
            self.wait(kind, 2, 0)
            for half in range(2):
                self.spread(kind, place.index(kind, 2, 0, half), False)

        def across(kind, along, step):
            self.wait(kind, along, step)
            near = 0 if step < 0 else 1
            self.start(kind, place.index(kind, along, step, near), place.device(kind, 0, -step))

        def across_opposite(kind, along):
            self.wait(kind, along, 2)

        result = []

        def add(blocks, function, *rest):
            for kind in range(2):
                result.append((kind, blocks, functools.partial(function, kind, *rest)))

        add([(0, 0)], partner)
        add([(-1, 0)], side_relay, -1)
        add([(1, 0)], side_relay, 1)
        add([], side_spread, -1)
        add([], side_spread, 1)
        add([(0, -1)], across, 0, -1)
        add([(0, 1)], across, 0, 1)
        add([(2, 0)], opposite)
        for along in (-1, 1, 2):
            add([(along, -1)], across, along, -1)
            add([(along, 1)], across, along, 1)
            before = {-1: 0, 1: -1, 2: 1}[along]
            add([(before, 2)], across_opposite, before)
        add([(2, 2)], across_opposite, 2)
        return result

    def finish(self):
        for kind in range(2):
            sent(self.sent(kind, 31 if self.partner_piece else 30), self.send.at[kind], self.place)


GATHER_SEMS = [pltpu.SemaphoreType.DMA((2,)), pltpu.SemaphoreType.DMA((2, 16))]
CHUNKS = 8
CHUNK = 8192 // CHUNKS


class Rows:
    def __init__(self, place, whole, others, send, recv):
        self.place, self.whole, self.others, self.send, self.recv = place, whole, others, send, recv
        self.mine, self.pair = place.mp, (place.mp + 2) % 4
        self.other = place.other_block() % 4
        self.far = (self.other + 2) % 4

    def copy(self, owner, chunk, device, lane):
        rows = pl.ds(pl.multiple_of(owner * 128, 128), 128)
        block = self.whole.at[rows, pl.ds(chunk * CHUNK, CHUNK)]
        return self.move(block, block, self.recv.at[owner, chunk], device, lane)

    def move(self, source, target, semaphore, device, lane):
        return pltpu.make_async_remote_copy(
            src_ref=source,
            dst_ref=target,
            send_sem=self.send.at[lane],
            recv_sem=semaphore,
            device_id=device,
            device_id_type=MESH,
        )

    def across(self, owner, chunk, device, lane, forward):
        rows = pl.ds(pl.multiple_of(owner * 128, 128), 128)
        for at in range(2):
            block = self.others.at[chunk * 2 + at, rows, :]
            source = block
            if not forward:
                first = pl.multiple_of((chunk * 2 + at) * 512 + (1 - self.place.h) * 256, 256)
                source = self.whole.at[rows, pl.ds(first, 256)]
            self.move(source, block, self.recv.at[4 + owner, chunk], device, lane).start()

    def own(self, chunk):
        self.copy(self.mine, chunk, self.place.pair_chip(), 0).start()
        self.copy(self.mine, chunk, self.place.core_partner(), 1).start()
        self.across(self.mine, chunk, self.place.other_chip(), 2, False)

    def arrive_pair(self, chunk):
        self.copy(self.pair, chunk, self.place.core_partner(), 0).wait_recv()
        self.copy(self.pair, chunk, self.place.core_partner(), 3).start()
        self.across(self.pair, chunk, self.place.other_chip(), 4, False)

    def wait_across(self, owner, chunk):
        amount = self.others.at[0, pl.ds(0, 256), :]
        self.move(amount, amount, self.recv.at[4 + owner, chunk], self.place.core_partner(), 0).wait_recv()

    def arrive_across(self, chunk):
        for owner, lane in ((self.other, 5), (self.far, 6)):
            self.wait_across(owner, chunk)
            self.across(owner, chunk, self.place.core_partner(), lane, True)

    def rest(self, chunk):
        for owner in (self.mine, self.pair):
            twin = owner + 1 - 2 * (owner % 2)
            self.copy(twin, chunk, self.place.core_partner(), 0).wait_recv()

    def rest_across(self, chunk):
        for owner in (self.other, self.far):
            self.wait_across(owner + 1 - 2 * (owner % 2), chunk)

    def finish(self):
        for lane in range(7):
            amount = self.whole.at[pl.ds(0, 128), :] if lane in (0, 1, 3) else self.others.at[:, pl.ds(0, 128), :]
            sent(amount, self.send.at[lane], self.place)


ROWS_SEMS = [pltpu.SemaphoreType.DMA((7,)), pltpu.SemaphoreType.DMA((8, CHUNKS))]


class Scatter:
    def __init__(self, place, part, land, send, recv):
        self.place, self.part, self.land, self.send, self.recv = place, part, land, send, recv

    def own(self, kind, along, across, half):
        block = self.place.index(kind, along, across, 0) // 2
        return self.part.at[block, pl.ds((half * 2 + kind) * 128, 128), :]

    def copy(self, kind, block, spot, device):
        return pltpu.make_async_remote_copy(
            src_ref=block,
            dst_ref=self.land.at[kind, spot],
            send_sem=self.send.at[kind],
            recv_sem=self.recv.at[kind, self.lane(spot)],
            device_id=device,
            device_id_type=MESH,
        )

    @staticmethod
    def lane(spot):
        if 16 <= spot < 24:
            return spot - 8
        return spot - 2 if spot in (28, 29) else spot

    def start(self, kind, block, spot, device):
        self.copy(kind, block, spot, device).start()

    def wait(self, kind, spots):
        amount = self.land.at[kind, pl.ds(0, len(spots))]
        pltpu.make_async_remote_copy(
            src_ref=amount,
            dst_ref=amount,
            send_sem=self.send.at[kind],
            recv_sem=self.recv.at[kind, self.lane(spots[0])],
            device_id=self.place.partner(),
            device_id_type=MESH,
        ).wait_recv()

    def add(self, kind, block, spots):
        self.wait(kind, spots)

        def step(at, carry):
            rows = pl.ds(pl.multiple_of(at * 64, 64), 64)
            total = block[rows, :].astype(jnp.float32)
            for spot in spots:
                total = total + self.land[kind, spot, rows, :].astype(jnp.float32)
            block[rows, :] = total.astype(jnp.bfloat16)
            return carry

        lax.fori_loop(0, 2, step, 0)

    def first(self, kind, offsets):
        for across in offsets:
            for half, along in ((0, 1), (1, -1)):
                block = self.own(kind, 2, across, half)
                self.start(kind, block, half * 4 + across, self.place.device(kind, along, 0))

    def second_own(self, kind, across):
        for side, along in ((0, 1), (1, -1)):
            half = 1 - side
            block = self.own(kind, along, across, half)
            spot = 8 + side * 8 + across * 2 + half
            self.start(kind, block, spot, self.place.device(kind, along, 0))

    def second(self, kind, across):
        for side, along in ((0, 1), (1, -1)):
            half = side
            block = self.own(kind, along, across, half)
            self.add(kind, block, [side * 4 + across])
            spot = 8 + side * 8 + across * 2 + half
            self.start(kind, block, spot, self.place.device(kind, along, 0))

    def third(self, kind, across):
        for half in range(2):
            block = self.own(kind, 0, across, half)
            self.add(kind, block, [8 + across * 2 + half, 16 + across * 2 + half])
            if across == 2:
                along = 1 if half == 0 else -1
                self.start(kind, block, 24 + half, self.place.device(kind, 0, along))
            if across in (1, 3):
                side = 0 if across == 1 else 1
                if half != side:
                    along = 1 if side == 0 else -1
                    self.start(kind, block, 26 + side * 2 + half, self.place.device(kind, 0, along))

    def fourth(self, kind):
        for side, across in ((0, 1), (1, 3)):
            block = self.own(kind, 0, across, side)
            self.add(kind, block, [24 + side])
            along = 1 if side == 0 else -1
            self.start(kind, block, 26 + side * 2 + side, self.place.device(kind, 0, along))

    def fifth(self, kind, grad):
        for half in range(2):
            self.wait_last(kind, half)
            grad[kind, :, half * 128 : (half + 1) * 128] = self.summed(kind, half).T

    def wait_last(self, kind, half):
        amount = self.land.at[kind, pl.ds(0, 2)]
        pltpu.make_async_remote_copy(
            src_ref=amount,
            dst_ref=amount,
            send_sem=self.send.at[kind],
            recv_sem=self.recv.at[kind, 26 + half],
            device_id=self.place.partner(),
            device_id_type=MESH,
        ).wait_recv()

    def summed(self, kind, half):
        total = self.own(kind, 0, 0, half)[...].astype(jnp.float32)
        for side in range(2):
            total = total + self.land[kind, 26 + side * 2 + half].astype(jnp.float32)
        return total

    def finish(self):
        for kind in range(2):
            sent(self.land.at[kind], self.send.at[kind], self.place)


FACTOR = HEAD ** (-0.5)
EXPONENT = FACTOR * 1.4426950408889634
F32 = jnp.float32
BF16 = jnp.bfloat16


def product(left, right):
    return jnp.dot(left, right, preferred_element_type=F32)


def product_rows(left, right):
    return lax.dot_general(left, right, (((1,), (1,)), ((), ())), preferred_element_type=F32)


def turn(field, cosine, sine):
    parts = []
    for head in range(field.shape[1] // HEAD):
        one = field[:, head * HEAD : (head + 1) * HEAD]
        parts.append(one * cosine + pltpu.roll(one, HEAD // 2, 1) * sine)
    return jnp.concatenate(parts, axis=1)


def softmax_down(keys, queries):
    scores = product_rows(keys, queries)
    ahead = lax.broadcasted_iota(jnp.int32, (256, 256), 0) > lax.broadcasted_iota(jnp.int32, (256, 256), 1)
    own = jnp.where(ahead, -jnp.inf, scores[-256:])
    scores = own if scores.shape[0] == 256 else jnp.concatenate([scores[:-256], own], axis=0)
    highest = jnp.max(scores, axis=0, keepdims=True)
    raised = jnp.exp2((scores - highest) * EXPONENT)
    return raised * (1.0 / jnp.sum(raised, axis=0, keepdims=True))


def columns(head):
    return pl.ds(pl.multiple_of(head * HEAD, HEAD), HEAD)


def base_heads(head, count, query, cotangent, keys, values, key_sum, value_sum):
    group = head // 8
    for block in range(2):
        rows, upto = pl.ds(block * 256, 256), (block + 1) * 256
        key_part, value_part = 0.0, 0.0
        for at in range(count):
            queries, pulls = query[rows, columns(head + at)], cotangent[rows, columns(head + at)]
            weights = softmax_down(keys[:upto, columns(group)], queries)
            pulled = product_rows(values[:upto, columns(group)], pulls)
            mean = jnp.sum(weights * pulled, axis=0, keepdims=True)
            back = (weights * (pulled - mean) * FACTOR).astype(BF16)
            value_part = value_part + product(weights.astype(BF16), pulls)
            key_part = key_part + product(back, queries)
        value_sum[:upto, columns(group)] += value_part
        key_sum[:upto, columns(group)] += key_part


def tangent_head(head, query, tangent, keys, key_tangent, turned, context, context_tangent):
    group = head // 8
    for block in range(2):
        rows, count = pl.ds(block * 256, 256), (block + 1) * 256
        queries = query[rows, columns(head)]
        weights = softmax_down(keys[:count, columns(group)], queries)
        both_keys = jnp.concatenate([keys[:count, columns(group)], key_tangent[:count, columns(group)]], axis=1)
        both_queries = jnp.concatenate([tangent[rows, columns(head)], queries], axis=1)
        spread = product_rows(both_keys, both_queries)
        mean = jnp.sum(weights * spread, axis=0, keepdims=True)
        moved = (weights * (spread - mean) * FACTOR).astype(BF16)
        first = product(turned[group, :, :count], weights.astype(BF16))
        second = product(turned[group, :HEAD, :count], moved)
        context[rows, columns(head)] = first[:HEAD].T.astype(BF16)
        context_tangent[rows, columns(head)] = (first[HEAD:] + second).T.astype(BF16)


def project(normed, weights, total, first, last):
    def step(at, carry):
        for kind, weight in enumerate(weights):
            sums = 0.0
            for part in range(4):
                index = at * 4 + part
                left = normed[:, pl.ds(pl.multiple_of(index * 256, 256), 256)]
                sums = sums + product(left, weight[index])
            total[:, kind * 256 : (kind + 1) * 256] += sums
        return carry

    lax.fori_loop(first, last, step, 0)


def project_half(left, weight, total):
    total[...] = jnp.zeros_like(total)

    def step(at, carry):
        for kind in range(2):
            sums = 0.0
            for part in range(4):
                sums = sums + product(left(at * 4 + part), weight[at * 4 + part, kind])
            total[:, kind * 256 : (kind + 1) * 256] += sums
        return carry

    lax.fori_loop(0, 4, step, 0)


def layer_kernel(
    tokens, gain, query_in, tangent_in, kv_in, bias, task_in, bias_task, cotangent_in, cosine, sine,
    context_out, context_tangent_out, grad, bias_grad,
    context, context_tangent, token_rows, query, tangent, cotangent, normed, other_rows, base_all, task_all, part, land, total,
    keys, values, kv_tangent, tangent_out, tangent_in_land, turned, key_sum, value_sum, back, back_other, sums, sums_land,
    local, out_sems, base_send, base_recv, task_send, task_recv, rows_send, rows_recv,
    part_send, part_recv, sums_send, sums_recv, pass_send, pass_recv,
):
    place = Place()
    h = place.h

    def load(source, target, at):
        copy = pltpu.make_async_copy(source, target, local.at[at])
        copy.start()
        return copy

    waits = [load(kv_in.at[kind], base_all.at[kind, place.dp], kind) for kind in range(2)]
    waits.append(load(task_in, task_all.at[place.dp // 2], 2))
    load_tokens = load(tokens, token_rows, 4)
    later = [load(query_in, query, 5), load(cotangent_in, cotangent, 6), load(tangent_in, tangent, 7)]
    around = ring_devices(place) + [place.core_partner(), place.pair_chip(), place.other_chip()]
    greet(around)

    def base_piece(kind, index):
        return base_all.at[kind, index]

    def task_piece(kind, index):
        return task_all.at[index // 2, kind, pl.ds(pl.multiple_of(index % 2 * 128, 128), 128), :]

    def task_sent(kind, count):
        return task_all.at[pl.ds(0, count // 2), kind]

    base = Gather(
        place, base_piece, lambda kind: base_piece(kind, place.dp),
        lambda kind, count: base_all.at[kind, pl.ds(0, count)], base_send, base_recv,
    )
    task = Gather(place, task_piece, None, task_sent, task_send, task_recv)
    rows = Rows(place, normed, other_rows, rows_send, rows_recv)
    for copy in waits:
        copy.wait()
    greeted(around)
    base.swap()
    base.first()
    load_tokens.wait()
    scale = gain[...]

    def norm(at, carry):
        here = pl.multiple_of(at * 16, 16)
        wide = token_rows[pl.ds(here, 16), :].astype(F32)
        mean = jnp.mean(wide * wide, axis=-1, keepdims=True)
        there = pl.multiple_of(rows.mine * 128 + here, 16)
        normed[pl.ds(there, 16), :] = (wide * lax.rsqrt(mean + 1e-06) * scale).astype(BF16)
        return carry

    lax.fori_loop(0, 8, norm, 0)
    for chunk in range(CHUNKS):
        rows.own(chunk)
    for copy in later:
        copy.wait()

    for at, (_, _, event) in enumerate(base.events()):
        event()
        if at in (16, 19, 22, 26, 31):
            chunk = (16, 19, 22, 26, 31).index(at)
            rows.arrive_pair(chunk)
    task.first()
    ahead = [event for _, _, event in task.events()]

    def events(count):
        for _ in range(min(count, len(ahead))):
            ahead.pop(0)()

    events(2)
    total[...] = jnp.zeros_like(total)
    both = [base_all.at[0], base_all.at[1]]
    rows.arrive_pair(5)
    for chunk in range(4):
        rows.rest(chunk)
    project(normed, both, total, 0, 4)
    for chunk in (4, 5, 6, 7):
        if chunk >= 6:
            rows.arrive_pair(chunk)
        events((0, 0, 8, 4)[chunk - 4])
        rows.rest(chunk)
        project(normed, both, total, chunk, chunk + 1)
    keys[...] = turn(total[:, :256] + bias[0:1, :], cosine[...], sine[...]).astype(BF16)
    values[...] = (total[:, 256:] + bias[1:2, :]).astype(BF16)
    key_sum[...] = jnp.zeros_like(key_sum)
    value_sum[...] = jnp.zeros_like(value_sum)
    sums[0] = jnp.zeros_like(sums[0])
    back_swaps = []

    def swap(source, target, at):
        return pltpu.make_async_remote_copy(
            src_ref=source,
            dst_ref=target,
            send_sem=pass_send.at[at],
            recv_sem=pass_recv.at[at],
            device_id=place.partner(),
            device_id_type=MESH,
        )

    for part_of in range(4):
        base_heads(part_of * 4, 4, query, cotangent, keys, values, key_sum, value_sum)
        events((2, 6, 10, 4)[part_of])
        for chunk in (part_of * 2, part_of * 2 + 1):
            rows.arrive_across(chunk)
        if part_of % 2 == 1:
            group = part_of // 2
            pick = slice(group * HEAD, (group + 1) * HEAD)
            key_back = turn(key_sum[:, pick], cosine[...], -sine[...]).astype(BF16).astype(F32)
            value_back = value_sum[:, pick].astype(BF16).astype(F32)
            back[group * 256 : group * 256 + 128, :] = key_back.T.astype(BF16)
            back[group * 256 + 128 : (group + 1) * 256, :] = value_back.T.astype(BF16)
            here = pl.ds(group * 256, 256)
            back_swaps.append(swap(back.at[here, :], back_other.at[here, :], group))
            back_swaps[-1].start()
            sums[0, 0:1, pick] = jnp.sum(key_back, axis=0, keepdims=True)
            sums[0, 1:2, pick] = jnp.sum(value_back, axis=0, keepdims=True)

    odd_y, odd_z = place.y % 2, place.z % 2
    mates = [
        place.device(0, 1 - 2 * odd_y, 0),
        place.device(0, 2 * odd_y - 1, 0),
        place.device(1, 1 - 2 * odd_z, 0),
        place.device(1, 2 * odd_z - 1, 0),
        place.partner(),
    ]

    def mate_copy(at):
        return pltpu.make_async_remote_copy(
            src_ref=sums.at[at],
            dst_ref=sums_land.at[at],
            send_sem=sums_send.at[at],
            recv_sem=sums_recv.at[at],
            device_id=mates[at],
            device_id_type=MESH,
        )

    def mate_sum(at):
        mate_copy(at).wait()
        sums[at + 1] = sums[at] + sums_land[at]
        if at + 1 < 5:
            mate_copy(at + 1).start()

    mate_copy(0).start()
    events(len(ahead))

    for chunk in range(CHUNKS):
        rows.rest_across(chunk)
    project_half(lambda block: other_rows[block], task_all, total)
    tangent_out[...] = total[...].astype(BF16)
    tangent_swaps = []
    for kind in range(2):
        pick = pl.ds(kind * 256, 256)
        tangent_swaps.append(swap(tangent_out.at[:, pick], tangent_in_land.at[:, pick], 2 + kind))
        tangent_swaps[-1].start()
    mate_sum(0)

    def half_columns(block):
        return pl.ds(pl.multiple_of(block * 512 + h * 256, 256), 256)

    project_half(lambda block: normed[:, half_columns(block)], task_all, total)
    for copy in back_swaps:
        copy.wait_recv()

    scatter = Scatter(place, part, land, part_send, part_recv)

    def gradients(count, offsets):
        def step(at, carry):
            off_y, off_z = offsets(at)
            block = ((place.z + off_z) % 4) * 4 + (place.y + off_y) % 4
            own = product(back[...], normed[:, half_columns(block)])
            part[block] = (own + product(back_other[...], other_rows[block])).astype(BF16)
            return carry

        lax.fori_loop(0, count, step, 0)

    gradients(2, lambda at: (2, 2 + at))
    scatter.first(0, (2, 3))
    gradients(2, lambda at: (2, at))
    scatter.first(0, (1, 0))
    gradients(3, lambda at: (3 + at, 2))
    scatter.first(1, (2, 3, 1, 0))
    mate_sum(1)
    gradients(6, lambda at: (1 + 2 * (at // 3), 3 + at % 3))
    gradients(3, lambda at: (0, 3 + at))

    outs = []

    def tangents(start, count):
        def step(at, carry):
            tangent_head(start + at, query, tangent, keys, kv_tangent.at[0], turned, context, context_tangent)
            return carry

        lax.fori_loop(0, count, step, 0, unroll=count)
        pick = pl.ds(start * HEAD, count * HEAD)
        for source, target in ((context, context_out), (context_tangent, context_tangent_out)):
            outs.append(pltpu.make_async_copy(source.at[:, pick], target.at[:, pick], out_sems.at[len(outs)]))
            outs[-1].start()

    def second(across):
        for kind in range(2):
            scatter.second_own(kind, across)
        for kind in range(2):
            scatter.second(kind, across)

    second(2)
    second(3)
    second(1)
    mate_sum(2)
    def turn_values():
        for copy in tangent_swaps:
            copy.wait_recv()
        key = total[:, :256] + tangent_in_land[:, :256].astype(F32) + bias_task[0:1, :]
        kv_tangent[0] = turn(key, cosine[...], sine[...]).astype(BF16)
        value = total[:, 256:] + tangent_in_land[:, 256:].astype(F32) + bias_task[1:2, :]
        kv_tangent[1] = value.astype(BF16)
        for group in range(2):
            pick = slice(group * HEAD, (group + 1) * HEAD)
            turned[group, :HEAD, :] = values[:, pick].astype(F32).T.astype(BF16)
            turned[group, HEAD:, :] = kv_tangent[1, :, pick].astype(F32).T.astype(BF16)

    def third(across):
        for kind in range(2):
            scatter.third(kind, across)

    def third(across):
        for kind in range(2):
            scatter.third(kind, across)

    turn_values()
    tangents(0, 2)
    third(2)
    second(0)
    tangents(2, 4)
    third(3)
    third(1)
    mate_sum(3)
    for kind in range(2):
        scatter.fourth(kind)
    tangents(6, 4)
    third(0)
    tangents(10, 2)
    for kind in range(2):
        scatter.fifth(kind, grad)
    mate_sum(4)
    bias_grad[...] = sums[5, 0:2, :]
    tangents(12, 4)
    for copy in outs:
        copy.wait()
    scatter.finish()
    base.finish()
    task.finish()
    rows.finish()
    for copy in back_swaps + tangent_swaps:
        copy.wait_send()


def layer(*operands):
    vmem = pl.BlockSpec(memory_space=pltpu.VMEM)
    hbm = pl.BlockSpec(memory_space=pl.ANY)
    scratch = [
        pltpu.VMEM((512, 2048), BF16),
        pltpu.VMEM((512, 2048), BF16),
        pltpu.VMEM((128, 8192), BF16),
        pltpu.VMEM((512, 2048), BF16),
        pltpu.VMEM((512, 2048), BF16),
        pltpu.VMEM((512, 2048), BF16),
        pltpu.VMEM((512, 8192), BF16),
        pltpu.VMEM((16, 512, 256), BF16),
        pltpu.VMEM((2, 32, 256, 256), BF16),
        pltpu.VMEM((16, 2, 256, 256), BF16),
        pltpu.VMEM((16, 512, 256), BF16),
        pltpu.VMEM((2, 30, 128, 256), BF16),
        pltpu.VMEM((512, 512), F32),
        pltpu.VMEM((512, 256), BF16),
        pltpu.VMEM((512, 256), BF16),
        pltpu.VMEM((2, 512, 256), BF16),
        pltpu.VMEM((512, 512), BF16),
        pltpu.VMEM((512, 512), BF16),
        pltpu.VMEM((2, 256, 512), BF16),
        pltpu.VMEM((512, 256), F32),
        pltpu.VMEM((512, 256), F32),
        pltpu.VMEM((512, 512), BF16),
        pltpu.VMEM((512, 512), BF16),
        pltpu.VMEM((6, 8, 256), F32),
        pltpu.VMEM((5, 8, 256), F32),
        pltpu.SemaphoreType.DMA((8,)),
        pltpu.SemaphoreType.DMA((14,)),
        *GATHER_SEMS,
        *GATHER_SEMS,
        *ROWS_SEMS,
        pltpu.SemaphoreType.DMA((2,)),
        pltpu.SemaphoreType.DMA((2, 31)),
        pltpu.SemaphoreType.DMA((5,)),
        pltpu.SemaphoreType.DMA((5,)),
        pltpu.SemaphoreType.DMA((4,)),
        pltpu.SemaphoreType.DMA((4,)),
    ]
    return pl.pallas_call(
        layer_kernel,
        out_shape=(
            jax.ShapeDtypeStruct((512, 2048), BF16),
            jax.ShapeDtypeStruct((512, 2048), BF16),
            jax.ShapeDtypeStruct((2, 256, 256), F32),
            jax.ShapeDtypeStruct((2, 256), F32),
        ),
        in_specs=[hbm, vmem, hbm, hbm, hbm, vmem, hbm, vmem, hbm, vmem, vmem],
        out_specs=(hbm, hbm, vmem, vmem),
        scratch_shapes=scratch,
        compiler_params=pltpu.CompilerParams(
            collective_id=0, has_side_effects=True, vmem_limit_bytes=62 * 1024 * 1024
        ),
        name="layer",
    )(*operands)


def hand_over_kernel(context, context_tangent, grad, bias_grad, *rest):
    outs, held, loads, stores = rest[:4], rest[4:8], rest[8], rest[9]
    pieces = []
    for at in range(4):
        rows = pl.ds(at * 128, 128)
        for which, source in ((0, context), (1, context_tangent)):
            pieces.append((source.at[rows, :], held[which].at[rows, :], outs[which].at[rows, :]))
    pieces.append((grad, held[2], outs[2]))
    pieces.append((bias_grad, held[3], outs[3]))
    arriving = [pltpu.make_async_copy(a, b, loads.at[at]) for at, (a, b, _) in enumerate(pieces)]
    leaving = [pltpu.make_async_copy(b, c, stores.at[at]) for at, (_, b, c) in enumerate(pieces)]
    for copy in arriving:
        copy.start()
    for copy, after in zip(arriving, leaving):
        copy.wait()
        after.start()
    for copy in leaving:
        copy.wait()


def hand_over(*results):
    hbm = pl.BlockSpec(memory_space=pl.ANY)
    return pl.pallas_call(
        hand_over_kernel,
        out_shape=tuple(jax.ShapeDtypeStruct(one.shape, one.dtype) for one in results),
        in_specs=[hbm] * 4,
        out_specs=(hbm,) * 4,
        scratch_shapes=[pltpu.VMEM(one.shape, one.dtype) for one in results]
        + [pltpu.SemaphoreType.DMA((10,)), pltpu.SemaphoreType.DMA((10,))],
        compiler_params=pltpu.CompilerParams(vmem_limit_bytes=62 * 1024 * 1024),
        name="hand_over",
    )(*results)


def turning_tables():
    position = np.arange(512, dtype=np.float64)[:, None]
    frequency = 1000000.0 ** (-2.0 * np.arange(64) / 128)
    angle = position * frequency[None, :]
    cosine, sine = np.cos(angle), np.sin(angle)
    return (
        np.concatenate([cosine, cosine], axis=1).astype(np.float32),
        np.concatenate([-sine, sine], axis=1).astype(np.float32),
    )


def body(tokens, gain, query, query_tangent, kv_weight, kv_bias, kv_task, kv_bias_task, cotangent):
    cosine, sine = turning_tables()
    return hand_over(*layer(
        tokens, gain.reshape(1, -1), query, query_tangent, kv_weight, kv_bias, kv_task, kv_bias_task, cotangent,
        jnp.asarray(cosine), jnp.asarray(sine),
    ))


def solution(mesh):
    in_specs = (
        P(("dp", "mp"), None),
        P(),
        P("dp", "mp"),
        P("dp", "mp"),
        P(None, "dp", "mp"),
        P(None, "mp"),
        P(None, "dp", "mp"),
        P(None, "mp"),
        P("dp", "mp"),
    )
    out_specs = (P("dp", "mp"), P("dp", "mp"), P(None, "dp", "mp"), P(None, "mp"))
    return jax.shard_map(body, mesh=mesh, in_specs=in_specs, out_specs=out_specs, check_vma=False)
```

```python
import functools

import jax
import jax.numpy as jnp
import numpy as np
from jax import lax
from jax.experimental import pallas as pl
from jax.experimental.pallas import tpu as pltpu
from jax.sharding import PartitionSpec as P

HEAD = 128
MESH = pl.DeviceIdType.MESH


class Place:
    def __init__(self):
        dp = lax.axis_index("dp")
        self.mp = lax.axis_index("mp")
        self.z, self.y, self.h = dp // 8, (dp // 2) % 4, dp % 2
        self.dp = dp

    def index(self, kind, along, across, half):
        dy, dz = (along, across) if kind == 0 else (across, along)
        return ((self.z + dz + 4) % 4) * 8 + ((self.y + dy + 4) % 4) * 2 + half

    def device(self, kind, along, across):
        return (self.index(kind, along, across, self.h), self.mp)

    def partner(self):
        return (self.dp + 1 - 2 * self.h, self.mp)

    def core_partner(self):
        return (self.dp, self.mp + 1 - 2 * (self.mp % 2))

    def pair_chip(self):
        return (self.dp, (self.mp + 2) % 4)

    def other_block(self):
        x = (self.h * 2 + self.mp // 2 + 2 * (self.mp // 2) + 3) % 4
        return x * 2 + self.mp % 2

    def other_chip(self):
        block = self.other_block()
        return (self.dp - self.h + block // 4, block % 4)


def greet(devices):
    barrier = pltpu.get_barrier_semaphore()
    for device in devices:
        pl.semaphore_signal(barrier, inc=1, device_id=device, device_id_type=MESH)


def greeted(devices):
    pl.semaphore_wait(pltpu.get_barrier_semaphore(), len(devices))


def ring_devices(place):
    return [
        place.device(0, 1, 0),
        place.device(0, -1, 0),
        place.device(0, 0, 1),
        place.device(0, 0, -1),
        place.partner(),
    ]


def sent(amount, semaphore, place):
    pltpu.make_async_remote_copy(
        src_ref=amount,
        dst_ref=amount,
        send_sem=semaphore,
        recv_sem=semaphore,
        device_id=place.partner(),
        device_id_type=MESH,
    ).wait_send()


class Gather:
    def __init__(self, place, piece, partner_piece, sent, send, recv):
        self.place, self.piece, self.partner_piece, self.sent = place, piece, partner_piece, sent
        self.send, self.recv = send, recv

    def copy(self, kind, index, device, source=None):
        block = self.piece(kind, index)
        return pltpu.make_async_remote_copy(
            src_ref=block if source is None else source,
            dst_ref=block,
            send_sem=self.send.at[kind],
            recv_sem=self.recv.at[kind, index // 2],
            device_id=device,
            device_id_type=MESH,
        )

    def start(self, kind, index, device, source=None):
        self.copy(kind, index, device, source).start()

    def wait(self, kind, along, across):
        index = self.place.index(kind, along, across, 0)
        amount = self.sent(kind, 2)
        pltpu.make_async_remote_copy(
            src_ref=amount,
            dst_ref=amount,
            send_sem=self.send.at[kind],
            recv_sem=self.recv.at[kind, index // 2],
            device_id=self.place.partner(),
            device_id_type=MESH,
        ).wait_recv()

    def spread(self, kind, index, along):
        if along:
            self.start(kind, index, self.place.device(kind, 1, 0))
            self.start(kind, index, self.place.device(kind, -1, 0))
        self.start(kind, index, self.place.device(kind, 0, 1))
        self.start(kind, index, self.place.device(kind, 0, -1))

    def swap(self):
        for kind in range(2):
            self.start(kind, self.place.dp, self.place.partner(), self.partner_piece(kind))

    def first(self):
        own = self.place.dp
        for kind in range(2):
            self.spread(kind, own, True)

    def events(self):
        place = self.place

        def partner(kind):
            other = place.index(kind, 0, 0, 1 - place.h)
            if self.partner_piece is not None:
                self.copy(kind, other, place.partner()).wait_recv()
            self.spread(kind, other, True)

        def side_relay(kind, along):
            self.wait(kind, along, 0)
            near = 0 if along < 0 else 1
            self.start(kind, place.index(kind, along, 0, near), place.device(kind, -along, 0))

        def side_spread(kind, along):
            for half in range(2):
                self.spread(kind, place.index(kind, along, 0, half), False)

        def opposite(kind):
            self.wait(kind, 2, 0)
            for half in range(2):
                self.spread(kind, place.index(kind, 2, 0, half), False)

        def across(kind, along, step):
            self.wait(kind, along, step)
            near = 0 if step < 0 else 1
            self.start(kind, place.index(kind, along, step, near), place.device(kind, 0, -step))

        def across_opposite(kind, along):
            self.wait(kind, along, 2)

        result = []

        def add(blocks, function, *rest):
            for kind in range(2):
                result.append((kind, blocks, functools.partial(function, kind, *rest)))

        add([(0, 0)], partner)
        add([(-1, 0)], side_relay, -1)
        add([(1, 0)], side_relay, 1)
        add([], side_spread, -1)
        add([], side_spread, 1)
        add([(0, -1)], across, 0, -1)
        add([(0, 1)], across, 0, 1)
        add([(2, 0)], opposite)
        for along in (-1, 1, 2):
            add([(along, -1)], across, along, -1)
            add([(along, 1)], across, along, 1)
            before = {-1: 0, 1: -1, 2: 1}[along]
            add([(before, 2)], across_opposite, before)
        add([(2, 2)], across_opposite, 2)
        return result

    def finish(self):
        for kind in range(2):
            sent(self.sent(kind, 31 if self.partner_piece else 30), self.send.at[kind], self.place)


GATHER_SEMS = [pltpu.SemaphoreType.DMA((2,)), pltpu.SemaphoreType.DMA((2, 16))]
CHUNKS = 8
CHUNK = 8192 // CHUNKS


class Rows:
    def __init__(self, place, whole, others, send, recv):
        self.place, self.whole, self.others, self.send, self.recv = place, whole, others, send, recv
        self.mine, self.pair = place.mp, (place.mp + 2) % 4
        self.other = place.other_block() % 4
        self.far = (self.other + 2) % 4

    def copy(self, owner, chunk, device, lane):
        rows = pl.ds(pl.multiple_of(owner * 128, 128), 128)
        block = self.whole.at[rows, pl.ds(chunk * CHUNK, CHUNK)]
        return self.move(block, block, self.recv.at[owner, chunk], device, lane)

    def move(self, source, target, semaphore, device, lane):
        return pltpu.make_async_remote_copy(
            src_ref=source,
            dst_ref=target,
            send_sem=self.send.at[lane],
            recv_sem=semaphore,
            device_id=device,
            device_id_type=MESH,
        )

    def across(self, owner, chunk, device, lane, forward):
        rows = pl.ds(pl.multiple_of(owner * 128, 128), 128)
        for at in range(2):
            block = self.others.at[chunk * 2 + at, rows, :]
            source = block
            if not forward:
                first = pl.multiple_of((chunk * 2 + at) * 512 + (1 - self.place.h) * 256, 256)
                source = self.whole.at[rows, pl.ds(first, 256)]
            self.move(source, block, self.recv.at[4 + owner, chunk], device, lane).start()

    def own(self, chunk):
        self.copy(self.mine, chunk, self.place.pair_chip(), 0).start()
        self.copy(self.mine, chunk, self.place.core_partner(), 1).start()
        self.across(self.mine, chunk, self.place.other_chip(), 2, False)

    def arrive_pair(self, chunk):
        self.copy(self.pair, chunk, self.place.core_partner(), 0).wait_recv()
        self.copy(self.pair, chunk, self.place.core_partner(), 3).start()
        self.across(self.pair, chunk, self.place.other_chip(), 4, False)

    def wait_across(self, owner, chunk):
        amount = self.others.at[0, pl.ds(0, 256), :]
        self.move(amount, amount, self.recv.at[4 + owner, chunk], self.place.core_partner(), 0).wait_recv()

    def arrive_across(self, chunk):
        for owner, lane in ((self.other, 5), (self.far, 6)):
            self.wait_across(owner, chunk)
            self.across(owner, chunk, self.place.core_partner(), lane, True)

    def rest(self, chunk):
        for owner in (self.mine, self.pair):
            twin = owner + 1 - 2 * (owner % 2)
            self.copy(twin, chunk, self.place.core_partner(), 0).wait_recv()

    def rest_across(self, chunk):
        for owner in (self.other, self.far):
            self.wait_across(owner + 1 - 2 * (owner % 2), chunk)

    def finish(self):
        for lane in range(7):
            amount = self.whole.at[pl.ds(0, 128), :] if lane in (0, 1, 3) else self.others.at[:, pl.ds(0, 128), :]
            sent(amount, self.send.at[lane], self.place)


ROWS_SEMS = [pltpu.SemaphoreType.DMA((7,)), pltpu.SemaphoreType.DMA((8, CHUNKS))]


class Scatter:
    def __init__(self, place, part, land, send, recv):
        self.place, self.part, self.land, self.send, self.recv = place, part, land, send, recv

    def own(self, kind, along, across, half):
        block = self.place.index(kind, along, across, 0) // 2
        return self.part.at[block, pl.ds((half * 2 + kind) * 128, 128), :]

    def copy(self, kind, block, spot, device):
        return pltpu.make_async_remote_copy(
            src_ref=block,
            dst_ref=self.land.at[kind, spot],
            send_sem=self.send.at[kind],
            recv_sem=self.recv.at[kind, self.lane(spot)],
            device_id=device,
            device_id_type=MESH,
        )

    @staticmethod
    def lane(spot):
        if 16 <= spot < 24:
            return spot - 8
        return spot - 2 if spot in (28, 29) else spot

    def start(self, kind, block, spot, device):
        self.copy(kind, block, spot, device).start()

    def wait(self, kind, spots):
        amount = self.land.at[kind, pl.ds(0, len(spots))]
        pltpu.make_async_remote_copy(
            src_ref=amount,
            dst_ref=amount,
            send_sem=self.send.at[kind],
            recv_sem=self.recv.at[kind, self.lane(spots[0])],
            device_id=self.place.partner(),
            device_id_type=MESH,
        ).wait_recv()

    def add(self, kind, block, spots):
        self.wait(kind, spots)

        def step(at, carry):
            rows = pl.ds(pl.multiple_of(at * 64, 64), 64)
            total = block[rows, :].astype(jnp.float32)
            for spot in spots:
                total = total + self.land[kind, spot, rows, :].astype(jnp.float32)
            block[rows, :] = total.astype(jnp.bfloat16)
            return carry

        lax.fori_loop(0, 2, step, 0)

    def first(self, kind, offsets):
        for across in offsets:
            for half, along in ((0, 1), (1, -1)):
                block = self.own(kind, 2, across, half)
                self.start(kind, block, half * 4 + across, self.place.device(kind, along, 0))

    def second_own(self, kind, across):
        for side, along in ((0, 1), (1, -1)):
            half = 1 - side
            block = self.own(kind, along, across, half)
            spot = 8 + side * 8 + across * 2 + half
            self.start(kind, block, spot, self.place.device(kind, along, 0))

    def second(self, kind, across):
        for side, along in ((0, 1), (1, -1)):
            half = side
            block = self.own(kind, along, across, half)
            self.add(kind, block, [side * 4 + across])
            spot = 8 + side * 8 + across * 2 + half
            self.start(kind, block, spot, self.place.device(kind, along, 0))

    def third(self, kind, across):
        for half in range(2):
            block = self.own(kind, 0, across, half)
            self.add(kind, block, [8 + across * 2 + half, 16 + across * 2 + half])
            if across == 2:
                along = 1 if half == 0 else -1
                self.start(kind, block, 24 + half, self.place.device(kind, 0, along))
            if across in (1, 3):
                side = 0 if across == 1 else 1
                if half != side:
                    along = 1 if side == 0 else -1
                    self.start(kind, block, 26 + side * 2 + half, self.place.device(kind, 0, along))

    def fourth(self, kind):
        for side, across in ((0, 1), (1, 3)):
            block = self.own(kind, 0, across, side)
            self.add(kind, block, [24 + side])
            along = 1 if side == 0 else -1
            self.start(kind, block, 26 + side * 2 + side, self.place.device(kind, 0, along))

    def fifth(self, kind, grad):
        for half in range(2):
            self.wait_last(kind, half)
            grad[kind, :, half * 128 : (half + 1) * 128] = self.summed(kind, half).T

    def wait_last(self, kind, half):
        amount = self.land.at[kind, pl.ds(0, 2)]
        pltpu.make_async_remote_copy(
            src_ref=amount,
            dst_ref=amount,
            send_sem=self.send.at[kind],
            recv_sem=self.recv.at[kind, 26 + half],
            device_id=self.place.partner(),
            device_id_type=MESH,
        ).wait_recv()

    def summed(self, kind, half):
        total = self.own(kind, 0, 0, half)[...].astype(jnp.float32)
        for side in range(2):
            total = total + self.land[kind, 26 + side * 2 + half].astype(jnp.float32)
        return total

    def finish(self):
        for kind in range(2):
            sent(self.land.at[kind], self.send.at[kind], self.place)


FACTOR = HEAD ** (-0.5)
EXPONENT = FACTOR * 1.4426950408889634
F32 = jnp.float32
BF16 = jnp.bfloat16


def product(left, right):
    return jnp.dot(left, right, preferred_element_type=F32)


def product_rows(left, right):
    return lax.dot_general(left, right, (((1,), (1,)), ((), ())), preferred_element_type=F32)


def turn(field, cosine, sine):
    parts = []
    for head in range(field.shape[1] // HEAD):
        one = field[:, head * HEAD : (head + 1) * HEAD]
        parts.append(one * cosine + pltpu.roll(one, HEAD // 2, 1) * sine)
    return jnp.concatenate(parts, axis=1)


def softmax_down(keys, queries):
    scores = product_rows(keys, queries)
    ahead = lax.broadcasted_iota(jnp.int32, (256, 256), 0) > lax.broadcasted_iota(jnp.int32, (256, 256), 1)
    own = jnp.where(ahead, -jnp.inf, scores[-256:])
    scores = own if scores.shape[0] == 256 else jnp.concatenate([scores[:-256], own], axis=0)
    highest = jnp.max(scores, axis=0, keepdims=True)
    raised = jnp.exp2((scores - highest) * EXPONENT)
    return raised * (1.0 / jnp.sum(raised, axis=0, keepdims=True))


def columns(head):
    return pl.ds(pl.multiple_of(head * HEAD, HEAD), HEAD)


def base_heads(head, count, query, cotangent, keys, values, key_sum, value_sum):
    group = head // 8
    for block in range(2):
        rows, upto = pl.ds(block * 256, 256), (block + 1) * 256
        key_part, value_part = 0.0, 0.0
        for at in range(count):
            queries, pulls = query[rows, columns(head + at)], cotangent[rows, columns(head + at)]
            weights = softmax_down(keys[:upto, columns(group)], queries)
            pulled = product_rows(values[:upto, columns(group)], pulls)
            mean = jnp.sum(weights * pulled, axis=0, keepdims=True)
            back = (weights * (pulled - mean) * FACTOR).astype(BF16)
            value_part = value_part + product(weights.astype(BF16), pulls)
            key_part = key_part + product(back, queries)
        value_sum[:upto, columns(group)] += value_part
        key_sum[:upto, columns(group)] += key_part


def tangent_head(head, query, tangent, keys, key_tangent, turned, context, context_tangent):
    group = head // 8
    for block in range(2):
        rows, count = pl.ds(block * 256, 256), (block + 1) * 256
        queries = query[rows, columns(head)]
        weights = softmax_down(keys[:count, columns(group)], queries)
        both_keys = jnp.concatenate([keys[:count, columns(group)], key_tangent[:count, columns(group)]], axis=1)
        both_queries = jnp.concatenate([tangent[rows, columns(head)], queries], axis=1)
        spread = product_rows(both_keys, both_queries)
        mean = jnp.sum(weights * spread, axis=0, keepdims=True)
        moved = (weights * (spread - mean) * FACTOR).astype(BF16)
        first = product(turned[group, :, :count], weights.astype(BF16))
        second = product(turned[group, :HEAD, :count], moved)
        context[rows, columns(head)] = first[:HEAD].T.astype(BF16)
        context_tangent[rows, columns(head)] = (first[HEAD:] + second).T.astype(BF16)


def project(normed, weights, total, first, last):
    def step(at, carry):
        for kind, weight in enumerate(weights):
            sums = 0.0
            for part in range(4):
                index = at * 4 + part
                left = normed[:, pl.ds(pl.multiple_of(index * 256, 256), 256)]
                sums = sums + product(left, weight[index])
            total[:, kind * 256 : (kind + 1) * 256] += sums
        return carry

    lax.fori_loop(first, last, step, 0)


def project_half(left, weight, total):
    total[...] = jnp.zeros_like(total)

    def step(at, carry):
        for kind in range(2):
            sums = 0.0
            for part in range(4):
                sums = sums + product(left(at * 4 + part), weight[at * 4 + part, kind])
            total[:, kind * 256 : (kind + 1) * 256] += sums
        return carry

    lax.fori_loop(0, 4, step, 0)


def layer_kernel(
    tokens, gain, query_in, tangent_in, kv_in, bias, task_in, bias_task, cotangent_in, cosine, sine,
    context_out, context_tangent_out, grad, bias_grad,
    context, context_tangent, token_rows, query, tangent, cotangent, normed, other_rows, base_all, task_all, part, land, total,
    keys, values, kv_tangent, tangent_out, tangent_in_land, turned, key_sum, value_sum, back, back_other, sums, sums_land,
    local, out_sems, base_send, base_recv, task_send, task_recv, rows_send, rows_recv,
    part_send, part_recv, sums_send, sums_recv, pass_send, pass_recv,
):
    place = Place()
    h = place.h

    def load(source, target, at):
        copy = pltpu.make_async_copy(source, target, local.at[at])
        copy.start()
        return copy

    waits = [load(kv_in.at[kind], base_all.at[kind, place.dp], kind) for kind in range(2)]
    waits.append(load(task_in, task_all.at[place.dp // 2], 2))
    load_tokens = load(tokens, token_rows, 4)
    later = [load(query_in, query, 5), load(cotangent_in, cotangent, 6), load(tangent_in, tangent, 7)]
    around = ring_devices(place) + [place.core_partner(), place.pair_chip(), place.other_chip()]
    greet(around)

    def base_piece(kind, index):
        return base_all.at[kind, index]

    def task_piece(kind, index):
        return task_all.at[index // 2, kind, pl.ds(pl.multiple_of(index % 2 * 128, 128), 128), :]

    def task_sent(kind, count):
        return task_all.at[pl.ds(0, count // 2), kind]

    base = Gather(
        place, base_piece, lambda kind: base_piece(kind, place.dp),
        lambda kind, count: base_all.at[kind, pl.ds(0, count)], base_send, base_recv,
    )
    task = Gather(place, task_piece, None, task_sent, task_send, task_recv)
    rows = Rows(place, normed, other_rows, rows_send, rows_recv)
    for copy in waits:
        copy.wait()
    greeted(around)
    base.swap()
    base.first()
    load_tokens.wait()
    scale = gain[...]

    def norm(at, carry):
        here = pl.multiple_of(at * 16, 16)
        wide = token_rows[pl.ds(here, 16), :].astype(F32)
        mean = jnp.mean(wide * wide, axis=-1, keepdims=True)
        there = pl.multiple_of(rows.mine * 128 + here, 16)
        normed[pl.ds(there, 16), :] = (wide * lax.rsqrt(mean + 1e-06) * scale).astype(BF16)
        return carry

    lax.fori_loop(0, 8, norm, 0)
    for chunk in range(CHUNKS):
        rows.own(chunk)
    for copy in later:
        copy.wait()

    for at, (_, _, event) in enumerate(base.events()):
        event()
        if at in (16, 19, 22, 26, 31):
            chunk = (16, 19, 22, 26, 31).index(at)
            rows.arrive_pair(chunk)
    task.first()
    ahead = [event for _, _, event in task.events()]

    def events(count):
        for _ in range(min(count, len(ahead))):
            ahead.pop(0)()

    events(2)
    total[...] = jnp.zeros_like(total)
    both = [base_all.at[0], base_all.at[1]]
    rows.arrive_pair(5)
    for chunk in range(4):
        rows.rest(chunk)
    project(normed, both, total, 0, 4)
    for chunk in (4, 5, 6, 7):
        if chunk >= 6:
            rows.arrive_pair(chunk)
        events((0, 0, 8, 4)[chunk - 4])
        rows.rest(chunk)
        project(normed, both, total, chunk, chunk + 1)
    keys[...] = turn(total[:, :256] + bias[0:1, :], cosine[...], sine[...]).astype(BF16)
    values[...] = (total[:, 256:] + bias[1:2, :]).astype(BF16)
    key_sum[...] = jnp.zeros_like(key_sum)
    value_sum[...] = jnp.zeros_like(value_sum)
    sums[0] = jnp.zeros_like(sums[0])
    back_swaps = []

    def swap(source, target, at):
        return pltpu.make_async_remote_copy(
            src_ref=source,
            dst_ref=target,
            send_sem=pass_send.at[at],
            recv_sem=pass_recv.at[at],
            device_id=place.partner(),
            device_id_type=MESH,
        )

    for part_of in range(4):
        base_heads(part_of * 4, 4, query, cotangent, keys, values, key_sum, value_sum)
        events((2, 6, 10, 4)[part_of])
        for chunk in (part_of * 2, part_of * 2 + 1):
            rows.arrive_across(chunk)
        if part_of % 2 == 1:
            group = part_of // 2
            pick = slice(group * HEAD, (group + 1) * HEAD)
            key_back = turn(key_sum[:, pick], cosine[...], -sine[...]).astype(BF16).astype(F32)
            value_back = value_sum[:, pick].astype(BF16).astype(F32)
            back[group * 256 : group * 256 + 128, :] = key_back.T.astype(BF16)
            back[group * 256 + 128 : (group + 1) * 256, :] = value_back.T.astype(BF16)
            here = pl.ds(group * 256, 256)
            back_swaps.append(swap(back.at[here, :], back_other.at[here, :], group))
            back_swaps[-1].start()
            sums[0, 0:1, pick] = jnp.sum(key_back, axis=0, keepdims=True)
            sums[0, 1:2, pick] = jnp.sum(value_back, axis=0, keepdims=True)

    odd_y, odd_z = place.y % 2, place.z % 2
    mates = [
        place.device(0, 1 - 2 * odd_y, 0),
        place.device(0, 2 * odd_y - 1, 0),
        place.device(1, 1 - 2 * odd_z, 0),
        place.device(1, 2 * odd_z - 1, 0),
        place.partner(),
    ]

    def mate_copy(at):
        return pltpu.make_async_remote_copy(
            src_ref=sums.at[at],
            dst_ref=sums_land.at[at],
            send_sem=sums_send.at[at],
            recv_sem=sums_recv.at[at],
            device_id=mates[at],
            device_id_type=MESH,
        )

    def mate_sum(at):
        mate_copy(at).wait()
        sums[at + 1] = sums[at] + sums_land[at]
        if at + 1 < 5:
            mate_copy(at + 1).start()

    mate_copy(0).start()
    events(len(ahead))

    for chunk in range(CHUNKS):
        rows.rest_across(chunk)
    project_half(lambda block: other_rows[block], task_all, total)
    tangent_out[...] = total[...].astype(BF16)
    tangent_swaps = []
    for kind in range(2):
        pick = pl.ds(kind * 256, 256)
        tangent_swaps.append(swap(tangent_out.at[:, pick], tangent_in_land.at[:, pick], 2 + kind))
        tangent_swaps[-1].start()
    mate_sum(0)

    def half_columns(block):
        return pl.ds(pl.multiple_of(block * 512 + h * 256, 256), 256)

    project_half(lambda block: normed[:, half_columns(block)], task_all, total)
    for copy in back_swaps:
        copy.wait_recv()

    scatter = Scatter(place, part, land, part_send, part_recv)

    def gradients(count, offsets):
        def step(at, carry):
            off_y, off_z = offsets(at)
            block = ((place.z + off_z) % 4) * 4 + (place.y + off_y) % 4
            own = product(back[...], normed[:, half_columns(block)])
            part[block] = (own + product(back_other[...], other_rows[block])).astype(BF16)
            return carry

        lax.fori_loop(0, count, step, 0)

    gradients(2, lambda at: (2, 2 + at))
    scatter.first(0, (2, 3))
    gradients(2, lambda at: (2, at))
    scatter.first(0, (1, 0))
    gradients(3, lambda at: (3 + at, 2))
    scatter.first(1, (2, 3, 1, 0))
    mate_sum(1)
    gradients(6, lambda at: (1 + 2 * (at // 3), 3 + at % 3))
    gradients(3, lambda at: (0, 3 + at))

    outs = []

    def tangents(start, count):
        def step(at, carry):
            tangent_head(start + at, query, tangent, keys, kv_tangent.at[0], turned, context, context_tangent)
            return carry

        lax.fori_loop(0, count, step, 0, unroll=count)
        pick = pl.ds(start * HEAD, count * HEAD)
        for source, target in ((context, context_out), (context_tangent, context_tangent_out)):
            outs.append(pltpu.make_async_copy(source.at[:, pick], target.at[:, pick], out_sems.at[len(outs)]))
            outs[-1].start()

    def second(across):
        for kind in range(2):
            scatter.second_own(kind, across)
        for kind in range(2):
            scatter.second(kind, across)

    second(2)
    second(3)
    second(1)
    mate_sum(2)
    def turn_values():
        for copy in tangent_swaps:
            copy.wait_recv()
        key = total[:, :256] + tangent_in_land[:, :256].astype(F32) + bias_task[0:1, :]
        kv_tangent[0] = turn(key, cosine[...], sine[...]).astype(BF16)
        value = total[:, 256:] + tangent_in_land[:, 256:].astype(F32) + bias_task[1:2, :]
        kv_tangent[1] = value.astype(BF16)
        for group in range(2):
            pick = slice(group * HEAD, (group + 1) * HEAD)
            turned[group, :HEAD, :] = values[:, pick].astype(F32).T.astype(BF16)
            turned[group, HEAD:, :] = kv_tangent[1, :, pick].astype(F32).T.astype(BF16)

    def third(across):
        for kind in range(2):
            scatter.third(kind, across)

    def third(across):
        for kind in range(2):
            scatter.third(kind, across)

    turn_values()
    tangents(0, 2)
    third(2)
    second(0)
    tangents(2, 4)
    third(3)
    third(1)
    mate_sum(3)
    for kind in range(2):
        scatter.fourth(kind)
    tangents(6, 4)
    third(0)
    tangents(10, 2)
    tangents(12, 4)
    for kind in range(2):
        scatter.fifth(kind, grad)
    mate_sum(4)
    bias_grad[...] = sums[5, 0:2, :]
    for copy in outs:
        copy.wait()
    scatter.finish()
    base.finish()
    task.finish()
    rows.finish()
    for copy in back_swaps + tangent_swaps:
        copy.wait_send()


def layer(*operands):
    vmem = pl.BlockSpec(memory_space=pltpu.VMEM)
    hbm = pl.BlockSpec(memory_space=pl.ANY)
    scratch = [
        pltpu.VMEM((512, 2048), BF16),
        pltpu.VMEM((512, 2048), BF16),
        pltpu.VMEM((128, 8192), BF16),
        pltpu.VMEM((512, 2048), BF16),
        pltpu.VMEM((512, 2048), BF16),
        pltpu.VMEM((512, 2048), BF16),
        pltpu.VMEM((512, 8192), BF16),
        pltpu.VMEM((16, 512, 256), BF16),
        pltpu.VMEM((2, 32, 256, 256), BF16),
        pltpu.VMEM((16, 2, 256, 256), BF16),
        pltpu.VMEM((16, 512, 256), BF16),
        pltpu.VMEM((2, 30, 128, 256), BF16),
        pltpu.VMEM((512, 512), F32),
        pltpu.VMEM((512, 256), BF16),
        pltpu.VMEM((512, 256), BF16),
        pltpu.VMEM((2, 512, 256), BF16),
        pltpu.VMEM((512, 512), BF16),
        pltpu.VMEM((512, 512), BF16),
        pltpu.VMEM((2, 256, 512), BF16),
        pltpu.VMEM((512, 256), F32),
        pltpu.VMEM((512, 256), F32),
        pltpu.VMEM((512, 512), BF16),
        pltpu.VMEM((512, 512), BF16),
        pltpu.VMEM((6, 8, 256), F32),
        pltpu.VMEM((5, 8, 256), F32),
        pltpu.SemaphoreType.DMA((8,)),
        pltpu.SemaphoreType.DMA((14,)),
        *GATHER_SEMS,
        *GATHER_SEMS,
        *ROWS_SEMS,
        pltpu.SemaphoreType.DMA((2,)),
        pltpu.SemaphoreType.DMA((2, 31)),
        pltpu.SemaphoreType.DMA((5,)),
        pltpu.SemaphoreType.DMA((5,)),
        pltpu.SemaphoreType.DMA((4,)),
        pltpu.SemaphoreType.DMA((4,)),
    ]
    return pl.pallas_call(
        layer_kernel,
        out_shape=(
            jax.ShapeDtypeStruct((512, 2048), BF16),
            jax.ShapeDtypeStruct((512, 2048), BF16),
            jax.ShapeDtypeStruct((2, 256, 256), F32),
            jax.ShapeDtypeStruct((2, 256), F32),
        ),
        in_specs=[hbm, vmem, hbm, hbm, hbm, vmem, hbm, vmem, hbm, vmem, vmem],
        out_specs=(hbm, hbm, vmem, vmem),
        scratch_shapes=scratch,
        compiler_params=pltpu.CompilerParams(
            collective_id=0, has_side_effects=True, vmem_limit_bytes=62 * 1024 * 1024
        ),
        name="layer",
    )(*operands)


def hand_over_kernel(context, context_tangent, grad, bias_grad, *rest):
    outs, held, loads, stores = rest[:4], rest[4:8], rest[8], rest[9]
    pieces = []
    for at in range(4):
        rows = pl.ds(at * 128, 128)
        for which, source in ((0, context), (1, context_tangent)):
            pieces.append((source.at[rows, :], held[which].at[rows, :], outs[which].at[rows, :]))
    pieces.append((grad, held[2], outs[2]))
    pieces.append((bias_grad, held[3], outs[3]))
    arriving = [pltpu.make_async_copy(a, b, loads.at[at]) for at, (a, b, _) in enumerate(pieces)]
    leaving = [pltpu.make_async_copy(b, c, stores.at[at]) for at, (_, b, c) in enumerate(pieces)]
    for copy in arriving:
        copy.start()
    for copy, after in zip(arriving, leaving):
        copy.wait()
        after.start()
    for copy in leaving:
        copy.wait()


def hand_over(*results):
    hbm = pl.BlockSpec(memory_space=pl.ANY)
    return pl.pallas_call(
        hand_over_kernel,
        out_shape=tuple(jax.ShapeDtypeStruct(one.shape, one.dtype) for one in results),
        in_specs=[hbm] * 4,
        out_specs=(hbm,) * 4,
        scratch_shapes=[pltpu.VMEM(one.shape, one.dtype) for one in results]
        + [pltpu.SemaphoreType.DMA((10,)), pltpu.SemaphoreType.DMA((10,))],
        compiler_params=pltpu.CompilerParams(vmem_limit_bytes=62 * 1024 * 1024),
        name="hand_over",
    )(*results)


def turning_tables():
    position = np.arange(512, dtype=np.float64)[:, None]
    frequency = 1000000.0 ** (-2.0 * np.arange(64) / 128)
    angle = position * frequency[None, :]
    cosine, sine = np.cos(angle), np.sin(angle)
    return (
        np.concatenate([cosine, cosine], axis=1).astype(np.float32),
        np.concatenate([-sine, sine], axis=1).astype(np.float32),
    )


def body(tokens, gain, query, query_tangent, kv_weight, kv_bias, kv_task, kv_bias_task, cotangent):
    cosine, sine = turning_tables()
    return hand_over(*layer(
        tokens, gain.reshape(1, -1), query, query_tangent, kv_weight, kv_bias, kv_task, kv_bias_task, cotangent,
        jnp.asarray(cosine), jnp.asarray(sine),
    ))


def solution(mesh):
    in_specs = (
        P(("dp", "mp"), None),
        P(),
        P("dp", "mp"),
        P("dp", "mp"),
        P(None, "dp", "mp"),
        P(None, "mp"),
        P(None, "dp", "mp"),
        P(None, "mp"),
        P("dp", "mp"),
    )
    out_specs = (P("dp", "mp"), P("dp", "mp"), P(None, "dp", "mp"), P(None, "mp"))
    return jax.shard_map(body, mesh=mesh, in_specs=in_specs, out_specs=out_specs, check_vma=False)
```
